32 devices in a mesh: img: 8 (over y, x, core), row: 4 (over z).
Axes of the slice: x: 2, y: 2, z: 4, core: 2. Of those that a mesh axis runs over, the one named last changes fastest.
Arguments:
- latents: bfloat16 [64, 512, 1024], P('img', 'row'), may hold values from -6 to 6
- cotangent: bfloat16 [64, 512, 1024], P('img', 'row'), may hold values from -6 to 6
- slot_crops: int32 [64], P('img'), may hold values from 0 to 8, as said below
- ln1_scale: bfloat16 [1024], replicated, may hold values from 0.25 to 1.75
- ln1_offset: bfloat16 [1024], replicated, may hold values from -1.5 to 1.5
- qkv_weight: bfloat16 [1024, 3072], replicated, may hold values from -0.25 to 0.25
- out_weight: bfloat16 [1024, 1024], replicated, may hold values from -0.5 to 0.5
- out_bias: bfloat16 [1024], replicated, may hold values from -1.5 to 1.5
- ln2_scale: bfloat16 [1024], replicated, may hold values from 0.25 to 1.75
- ln2_offset: bfloat16 [1024], replicated, may hold values from -1.5 to 1.5
- up_weight: bfloat16 [1024, 1024], replicated, may hold values from -0.1875 to 0.1875
- up_bias: bfloat16 [1024], replicated, may hold values from -2.5 to 2.5
- down_weight: bfloat16 [1024, 1024], replicated, may hold values from -0.25 to 0.25
- down_bias: bfloat16 [1024], replicated, may hold values from -1.5 to 1.5
Outputs:
- block_out: bfloat16 [64, 512, 1024], P('img', 'row')
- latents_grad: bfloat16 [64, 512, 1024], P('img', 'row')
- ln1_scale_grad: float32 [1024], P(('img', 'row'))
- ln1_offset_grad: float32 [1024], P(('img', 'row'))
- qkv_weight_grad: float32 [1024, 3072], P(('img', 'row'))
- out_weight_grad: float32 [1024, 1024], P(('img', 'row'))
- out_bias_grad: float32 [1024], P(('img', 'row'))
- ln2_scale_grad: float32 [1024], P(('img', 'row'))
- ln2_offset_grad: float32 [1024], P(('img', 'row'))
- up_weight_grad: float32 [1024, 1024], P(('img', 'row'))
- up_bias_grad: float32 [1024], P(('img', 'row'))
- down_weight_grad: float32 [1024, 1024], P(('img', 'row'))
- down_bias_grad: float32 [1024], P(('img', 'row'))
The draws below stay inside these ranges and needn't reach their ends.
Inputs may be any that keep to these rules, and one draw needn't show every extreme that they name: `slot_crops`: A slot holds the number of crops of its image, 1 to 8, or 0 if it is empty. The full slots, in slot order, hold the images one after another, each image's crops in consecutive full slots; the first image has 8 crops in every draw. Each index of img holds at least one full slot, its empty slots stand after its full ones, the first index of img has no empty slot and the last at least one.
All inputs are finite; a program needn't handle non-finite values.
Results may differ from the reference program's by a relative error of at most 0.015.
Values may be sent and summed in bfloat16 or wider, within the bound.
A program may use at most 256 MiB of HBM per device.

```python
import math
import jax
import jax.numpy as jnp
from jax import lax

D = 1024
FF = 1024
HEADS = 8
LAT = 512
SLOTS_PER_SHARD = 8
SLOTS = 64


def draw_slot_crops(key, part):
    key = jax.random.fold_in(key, 11)
    vacant_key, count_key = jax.random.split(key)
    holder_count = SLOTS // SLOTS_PER_SHARD
    vacant_slots = jax.random.randint(vacant_key, (holder_count,), 0, SLOTS_PER_SHARD)
    vacant_slots = vacant_slots.at[0].set(0)
    vacant_slots = vacant_slots.at[holder_count - 1].set(jnp.maximum(vacant_slots[holder_count - 1], 1))
    positions = jnp.arange(SLOTS)
    within_shard_index = positions % SLOTS_PER_SHARD
    holder_index = positions // SLOTS_PER_SHARD
    filled_slot = (within_shard_index < SLOTS_PER_SHARD - vacant_slots[holder_index]).astype(jnp.int32)
    ranked = jnp.cumsum(filled_slot) - filled_slot
    full_total = jnp.sum(filled_slot)
    image_sizes = jax.random.randint(count_key, (SLOTS,), 1, 9).at[0].set(8)
    image_ends = jnp.cumsum(image_sizes)
    image_starts = image_ends - image_sizes
    image_of = jnp.sum((image_ends[None, :] <= ranked[:, None]).astype(jnp.int32), 1)
    matches = positions[None, :] == image_of[:, None]
    size_of = jnp.sum(jnp.where(matches, image_sizes[None, :], 0), 1)
    start_of = jnp.sum(jnp.where(matches, image_starts[None, :], 0), 1)
    crop_total = jnp.minimum(size_of, full_total - start_of)
    return jnp.where(filled_slot > 0, crop_total, 0).astype(jnp.int32)


def with_spikes(array, rng, source, target, shards_of, factor):
    owner, partner = [(jnp.arange(array.shape[dim]) // (array.shape[dim] // shards_of)).reshape([-1 if axis == dim else 1 for axis in range(array.ndim)]) for dim in (source, target)]
    chosen = jax.random.permutation(rng, shards_of)[partner]
    strong = (owner == chosen) | (owner == (partner + shards_of // 2) % shards_of)
    return jnp.where(strong, factor * array, array)


def steps_of(rng, shape, cuts, least, largest):
    gain = 1.0
    for axis_at, shards_of in cuts:
        draws = jax.random.uniform(jax.random.fold_in(jax.random.fold_in(rng, 6), axis_at), (shards_of,), jnp.float32, least / len(cuts), largest / len(cuts))
        gain = gain * jnp.repeat(jnp.exp(draws), shape[axis_at] // shards_of).reshape((-1,) + (1,) * (len(shape) - 1 - axis_at))
    return gain


def scatter_about(key, extent, scale, limit, cuts=(), held_as=jnp.bfloat16):
    values = scale * jax.random.normal(key, extent, jnp.float32)
    if cuts:
        values = values * steps_of(key, extent, cuts, -0.22, 0.18)
    return jnp.clip(values, -limit, limit).astype(held_as)


def noise_with(rng, shape, scale, limit, shards, heavy, kind=jnp.bfloat16):
    values = scale * jax.random.normal(rng, shape, jnp.float32)
    if shards:
        values = values * steps_of(rng, shape, shards, -0.22, 0.18)
    return jnp.clip(with_spikes(values, jax.random.fold_in(rng, 3), *heavy), -limit, limit).astype(kind)


def setup_inputs(seed: int = 0) -> dict:
    seeds = jax.random.split(jax.random.key(seed), 15)
    return {
        "latents": scatter_about(seeds[0], (SLOTS, LAT, D), 1.0, 6.0, ((0, 8), (1, 4))),
        "cotangent": noise_with(seeds[1], (SLOTS, LAT, D), 1.0, 6.0, ((0, 8), (1, 4)), (0, 2, 8, 2.0)),
        "slot_crops": draw_slot_crops(jax.random.fold_in(seeds[14], 71), 0),
        "ln1_scale": jnp.clip(1.0 + 0.15 * jax.random.normal(seeds[3], (D,), jnp.float32), 0.25, 1.75).astype(jnp.bfloat16),
        "ln1_offset": scatter_about(seeds[4], (D,), 0.3, 1.5),
        "qkv_weight": scatter_about(seeds[5], (D, 3 * D), (D // 2) ** -0.5, 0.25),
        "out_weight": scatter_about(seeds[6], (D, D), (D // 8) ** -0.5, 0.5),
        "out_bias": scatter_about(seeds[7], (D,), 0.3, 1.5),
        "ln2_scale": jnp.clip(1.0 + 0.15 * jax.random.normal(seeds[8], (D,), jnp.float32), 0.25, 1.75).astype(jnp.bfloat16),
        "ln2_offset": scatter_about(seeds[9], (D,), 0.3, 1.5),
        "up_weight": scatter_about(seeds[10], (D, FF), D ** -0.5, 0.1875),
        "up_bias": scatter_about(seeds[11], (FF,), 0.5, 2.5),
        "down_weight": scatter_about(seeds[12], (FF, D), (FF // 2) ** -0.5, 0.25),
        "down_bias": scatter_about(seeds[13], (D,), 0.3, 1.5),
    }


@jax.custom_vjp
def low(v):
    return lax.optimization_barrier(v.astype(jnp.bfloat16)).astype(jnp.float32)

@jax.custom_vjp
def low_back(v):
    return v

def low_keep(v):
    return (low(v), None)

def low_pass(kept, grad):
    return (grad,)

def back_keep(v):
    return (v, None)

def back_low(kept, grad):
    return (low(grad),)
low.defvjp(low_keep, low_pass)
low_back.defvjp(back_keep, back_low)
EPSILON = 1e-05
PRECISE = lax.Precision.HIGHEST

def layer_norm(values, scale, offset):
    row_mean = lax.optimization_barrier(jnp.mean(values, -1, keepdims=True))
    centred = values - row_mean
    variance = lax.optimization_barrier(jnp.mean(centred * centred, -1, keepdims=True))
    return centred * lax.rsqrt(variance + EPSILON) * scale + offset

def block(params, latents):
    scale_one, offset_one, qkv_weight, out_weight, out_bias, scale_two, offset_two, up_weight, up_bias, down_weight, down_bias = params
    crop_count = latents.shape[0]
    head_size = D // HEADS
    hidden_one = low(layer_norm(latents, scale_one, offset_one))
    qkv = low_back(low(jnp.einsum('cld,de->cle', hidden_one, qkv_weight, precision=PRECISE)))
    queries = qkv[..., :D].reshape(crop_count, LAT, HEADS, head_size)
    keys = qkv[..., D:2 * D].reshape(crop_count, LAT, HEADS, head_size)
    values = qkv[..., 2 * D:].reshape(crop_count, LAT, HEADS, head_size)
    scores = low_back(jnp.einsum('cqhd,ckhd->chqk', queries, keys, precision=PRECISE) * head_size ** (-0.5))
    probs = low(jax.nn.softmax(scores, axis=-1))
    mixed = jnp.einsum('chqk,ckhd->cqhd', probs, values, precision=PRECISE).reshape(crop_count, LAT, D)
    mixed = low_back(low(mixed))
    attended = low_back(jnp.einsum('cld,de->cle', mixed, out_weight, precision=PRECISE) + out_bias)
    resid = latents + attended
    hidden_two = low(layer_norm(resid, scale_two, offset_two))
    before = low_back(jnp.einsum('cld,df->clf', hidden_two, up_weight, precision=PRECISE) + up_bias)
    activated = low(jax.nn.gelu(before))
    branch = low_back(jnp.einsum('clf,fd->cld', activated, down_weight, precision=PRECISE) + down_bias)
    return resid + branch

def reference(latents, cotangent, slot_crops, ln1_scale, ln1_offset, qkv_weight, out_weight, out_bias, ln2_scale, ln2_offset, up_weight, up_bias, down_weight, down_bias):
    params = tuple((weight.astype(jnp.float32) for weight in (ln1_scale, ln1_offset, qkv_weight, out_weight, out_bias, ln2_scale, ln2_offset, up_weight, up_bias, down_weight, down_bias)))
    valid = slot_crops > 0
    share = jnp.where(valid, 1.0 / jnp.maximum(slot_crops, 1).astype(jnp.float32), 0.0).astype(jnp.float32)
    group = math.gcd(SLOTS, 8)
    steps_count = SLOTS // group
    crop_values = latents.astype(jnp.float32).reshape(steps_count, group, LAT, D)
    crop_grads = (cotangent.astype(jnp.float32) * share[:, None, None]).reshape(steps_count, group, LAT, D)

    def scan_step(totals, inputs):
        values, upstream = inputs
        result, pullback = jax.vjp(block, params, values)
        param_grads, input_grad = pullback(upstream)
        totals = jax.tree.map(jnp.add, totals, param_grads)
        return (totals, (result, input_grad))
    start_totals = jax.tree.map(jnp.zeros_like, params)
    totals, (results, input_grads) = lax.scan(scan_step, start_totals, (crop_values, crop_grads))
    results = results.reshape(SLOTS, LAT, D)
    block_out = jnp.where(valid[:, None, None], results, 0.0).astype(jnp.bfloat16)
    latents_grad = input_grads.reshape(SLOTS, LAT, D).astype(jnp.bfloat16)
    return (block_out, latents_grad, totals[0], totals[1], totals[2], totals[3], totals[4], totals[5], totals[6], totals[7], totals[8], totals[9], totals[10])
```

```python
import functools
import jax
import jax.numpy as jnp
from jax import lax
from jax.experimental import pallas as pl
from jax.experimental.pallas import tpu as pltpu
from jax.sharding import PartitionSpec as P

HEADS = 8
EPSILON = 1e-05
F32 = jnp.float32
BF16 = jnp.bfloat16
ANY = pl.BlockSpec(memory_space=pl.ANY)
VM = pl.BlockSpec(memory_space=pltpu.VMEM)
SM = pl.BlockSpec(memory_space=pltpu.SMEM)
VMEM_LIMIT = 60 * 1024 * 1024


def dot(a, b):
    return jnp.dot(a, b, preferred_element_type=F32)


def dot_t(a, b):
    return lax.dot_general(a, b, (((1,), (1,)), ((), ())), preferred_element_type=F32)


def dot_tt(a, b):
    return lax.dot_general(a, b, (((0,), (0,)), ((), ())), preferred_element_type=F32)


def norm_parts(values):
    mean = jnp.mean(values, -1, keepdims=True)
    centred = values - mean
    inverse = lax.rsqrt(jnp.mean(centred * centred, -1, keepdims=True) + EPSILON)
    return centred * inverse, inverse


GELU_A = 0.7978845608028654
GELU_B = 0.044715


def forward_kernel(
    pieces, rows, width,
    *refs,
):
    (full,), refs = refs[:1], refs[1:]
    xs, refs = refs[:pieces], refs[pieces:]
    (scale1, offset1, scale2, offset2, bias_o, bias_u, bias_d, w_qkv, w_o, w_u, w_d), refs = refs[:11], refs[11:]
    outs, refs = refs[:pieces], refs[pieces:]
    (h1_o, qkv_o, probs_o, mixed_o, resid_o, h2_o, pre_o, act_o), refs = refs[:8], refs[8:]
    (vq, vo, vu, vd, h1, qkv, probs, mixed, resid, h2, pre, act, in_sem, out_sem) = refs
    heads = HEADS
    size = width // heads
    chunk = rows // pieces
    loads = [
        pltpu.make_async_copy(a, b, in_sem.at[i])
        for i, (a, b) in enumerate(((w_qkv, vq), (w_o, vo), (w_u, vu), (w_d, vd)))
    ]
    for load in loads:
        load.start()
    saves = [
        pltpu.make_async_copy(a, b, out_sem.at[i])
        for i, (a, b) in enumerate(
            ((h1, h1_o), (qkv, qkv_o), (probs, probs_o), (mixed, mixed_o), (resid, resid_o), (h2, h2_o), (pre, pre_o), (act, act_o))
        )
    ]
    s1, o1 = scale1[...].astype(F32), offset1[...].astype(F32)
    for i, x in enumerate(xs):
        hat, _ = norm_parts(x[...].astype(F32))
        h1[pl.ds(i * chunk, chunk), :] = (hat * s1 + o1).astype(BF16)
    saves[0].start()
    loads[0].wait()

    @pl.loop(0, 3 * width // 256)
    def _(n):
        cols = pl.ds(pl.multiple_of(n * 256, 256), 256)
        qkv[:, cols] = dot(h1[...], vq[:, cols]).astype(BF16)

    saves[1].start()
    factor = size ** -0.5 * 1.4426950408889634

    for h in range(heads):
        q = qkv[:, h * size:(h + 1) * size]
        k = qkv[:, width + h * size:width + (h + 1) * size]
        v = qkv[:, 2 * width + h * size:2 * width + (h + 1) * size]
        s = dot_t(k, q)
        top = jnp.max(s, 0, keepdims=True)
        e = jnp.exp2((s - top) * factor)
        p = (e * (1.0 / jnp.sum(e, 0, keepdims=True))).astype(BF16)
        probs[h] = p
        o = dot(v.T, p)
        mixed[:, h * size:(h + 1) * size] = o.T.astype(BF16)
    saves[2].start()
    saves[3].start()
    loads[1].wait()
    bo = bias_o[...].astype(F32)
    s2, o2 = scale2[...].astype(F32), offset2[...].astype(F32)
    for i, x in enumerate(xs):
        part = pl.ds(i * chunk, chunk)
        r = x[...].astype(F32) + dot(mixed[part, :], vo[...]) + bo
        resid[part, :] = r
        hat, _ = norm_parts(r)
        h2[part, :] = (hat * s2 + o2).astype(BF16)
    saves[4].start()
    saves[5].start()
    loads[2].wait()
    bu = bias_u[...].astype(F32)
    for i in range(pieces):
        part = pl.ds(i * chunk, chunk)
        u = dot(h2[part, :], vu[...]) + bu
        pre[part, :] = u
        act[part, :] = (0.5 * u * (1.0 + jnp.tanh(GELU_A * (u + GELU_B * u * u * u)))).astype(BF16)
    saves[6].start()
    saves[7].start()
    loads[3].wait()
    bd = bias_d[...].astype(F32)
    keep = full[0] > 0
    for i in range(pieces):
        part = pl.ds(i * chunk, chunk)
        out = resid[part, :] + dot(act[part, :], vd[...]) + bd
        outs[i][...] = jnp.where(keep, out, 0.0).astype(BF16)
    for save in saves:
        save.wait()


def forward(full, xs, vecs, mats):
    pieces = len(xs)
    chunk, width = xs[0].shape
    rows = chunk * pieces
    sds = jax.ShapeDtypeStruct
    saved = [
        sds((rows, width), BF16), sds((rows, 3 * width), BF16), sds((HEADS, rows, rows), BF16), sds((rows, width), BF16),
        sds((rows, width), F32), sds((rows, width), BF16), sds((rows, width), F32), sds((rows, width), BF16),
    ]
    out_shape = [sds((chunk, width), BF16)] * pieces + saved
    macs = rows * width * width * 6 + 2 * rows * rows * width
    res = pl.pallas_call(
        functools.partial(forward_kernel, pieces, rows, width),
        out_shape=out_shape,
        in_specs=[SM] + [VM] * pieces + [VM] * 7 + [ANY] * 4,
        out_specs=[VM] * pieces + [ANY] * 8,
        scratch_shapes=[
            pltpu.VMEM((width, 3 * width), BF16), pltpu.VMEM((width, width), BF16), pltpu.VMEM((width, width), BF16), pltpu.VMEM((width, width), BF16),
        ] + [pltpu.VMEM(s.shape, s.dtype) for s in saved] + [pltpu.SemaphoreType.DMA((4,)), pltpu.SemaphoreType.DMA((8,))],
        compiler_params=pltpu.CompilerParams(vmem_limit_bytes=VMEM_LIMIT),
        cost_estimate=pl.CostEstimate(flops=2 * macs, bytes_accessed=32 << 20, transcendentals=0),
        name="slot_forward",
    )(full, *xs, *vecs, *mats)
    return res[:pieces], res[pieces:]


def backward_kernel(pieces, rows, width, *refs):
    (share,), refs = refs[:1], refs[1:]
    cots, refs = refs[:pieces], refs[pieces:]
    xs, refs = refs[:pieces], refs[pieces:]
    (scale1, scale2), refs = refs[:2], refs[2:]
    hbm_in, refs = refs[:9], refs[9:]
    outs, refs = refs[:pieces], refs[pieces:]
    (sums_o,), refs = refs[:1], refs[1:]
    (gl_o, gp_o, ga_o, gqkv_o), refs = refs[:4], refs[4:]
    (vd, pre, vu, resid, vo, qkv, probs, vq, _unused), refs = refs[:9], refs[9:]
    (gl, gp, ga, gqkv, gm, gres, sums, in_sem, out_sem) = refs
    size = width // HEADS
    chunk = rows // pieces
    vm_in = (vd, pre, vu, resid, vo, qkv, probs, vq)
    loads = [pltpu.make_async_copy(a, b, in_sem.at[i]) for i, (a, b) in enumerate(zip(hbm_in[:8], vm_in))]
    for load in loads:
        load.start()
    saves = [
        pltpu.make_async_copy(a, b, out_sem.at[i])
        for i, (a, b) in enumerate(((gl, gl_o), (gp, gp_o), (ga, ga_o), (gqkv, gqkv_o)))
    ]
    part_share = share[0]
    bias_d = jnp.zeros((1, width), F32)
    for i in range(pieces):
        part = pl.ds(i * chunk, chunk)
        g = (cots[i][...].astype(F32) * part_share).astype(BF16)
        gl[part, :] = g
        bias_d = bias_d + jnp.sum(g.astype(F32), 0, keepdims=True)
    sums[0:1, :] = bias_d
    saves[0].start()
    loads[0].wait()
    loads[1].wait()
    bias_u = jnp.zeros((1, width), F32)
    for i in range(pieces):
        part = pl.ds(i * chunk, chunk)
        ga_ = dot_t(gl[part, :], vd[...])
        u = pre[part, :]
        t = jnp.tanh(GELU_A * (u + GELU_B * u * u * u))
        slope = 0.5 * (1.0 + t) + 0.5 * u * (1.0 - t * t) * (GELU_A * (1.0 + 3.0 * GELU_B * u * u))
        g = (ga_ * slope).astype(BF16)
        gp[part, :] = g
        bias_u = bias_u + jnp.sum(g.astype(F32), 0, keepdims=True)
    sums[1:2, :] = bias_u
    saves[1].start()
    loads[2].wait()
    loads[3].wait()
    s2 = scale2[...].astype(F32)
    scale_g = jnp.zeros((1, width), F32)
    offset_g = jnp.zeros((1, width), F32)
    bias_o = jnp.zeros((1, width), F32)
    for i in range(pieces):
        part = pl.ds(i * chunk, chunk)
        gh = dot_t(gp[part, :], vu[...])
        hat, inverse = norm_parts(resid[part, :])
        scale_g = scale_g + jnp.sum(gh * hat, 0, keepdims=True)
        offset_g = offset_g + jnp.sum(gh, 0, keepdims=True)
        e = gh * s2
        gr = cots[i][...].astype(F32) * part_share + inverse * (
            e - jnp.mean(e, -1, keepdims=True) - hat * jnp.mean(e * hat, -1, keepdims=True)
        )
        gres[part, :] = gr
        g = gr.astype(BF16)
        ga[part, :] = g
        bias_o = bias_o + jnp.sum(g.astype(F32), 0, keepdims=True)
    sums[2:3, :] = scale_g
    sums[3:4, :] = offset_g
    sums[4:5, :] = bias_o
    saves[2].start()
    loads[4].wait()
    for i in range(pieces):
        part = pl.ds(i * chunk, chunk)
        gm[part, :] = dot_t(ga[part, :], vo[...]).astype(BF16)
    loads[5].wait()
    loads[6].wait()
    factor = size ** -0.5
    for h in range(HEADS):
        qc = slice(h * size, (h + 1) * size)
        kc = slice(width + h * size, width + (h + 1) * size)
        vc = slice(2 * width + h * size, 2 * width + (h + 1) * size)
        q, k, v, m = qkv[:, qc], qkv[:, kc], qkv[:, vc], gm[:, qc]
        p = probs[h]
        dp = dot_t(v, m)
        pf = p.astype(F32)
        w = pf * dp
        ds = (w - pf * jnp.sum(w, 0, keepdims=True)).astype(BF16)
        gqkv[:, vc] = dot(p, m).astype(BF16)
        gqkv[:, kc] = (dot(ds, q) * factor).astype(BF16)
        gqkv[:, qc] = (dot(k.T, ds) * factor).T.astype(BF16)
    saves[3].start()
    loads[7].wait()
    s1 = scale1[...].astype(F32)
    scale_g = jnp.zeros((1, width), F32)
    offset_g = jnp.zeros((1, width), F32)
    for i in range(pieces):
        part = pl.ds(i * chunk, chunk)
        gh = dot_t(gqkv[part, :], vq[...])
        hat, inverse = norm_parts(xs[i][...].astype(F32))
        scale_g = scale_g + jnp.sum(gh * hat, 0, keepdims=True)
        offset_g = offset_g + jnp.sum(gh, 0, keepdims=True)
        e = gh * s1
        outs[i][...] = (
            gres[part, :] + inverse * (e - jnp.mean(e, -1, keepdims=True) - hat * jnp.mean(e * hat, -1, keepdims=True))
        ).astype(BF16)
    sums[5:6, :] = scale_g
    sums[6:7, :] = offset_g
    sums[7:8, :] = jnp.zeros((1, width), F32)
    sums_o[...] = sums[...]
    for save in saves:
        save.wait()


def backward(share, cots, xs, vecs, hbm_in):
    pieces = len(xs)
    chunk, width = xs[0].shape
    rows = chunk * pieces
    sds = jax.ShapeDtypeStruct
    saved = [sds((rows, width), BF16), sds((rows, width), BF16), sds((rows, width), BF16), sds((rows, 3 * width), BF16)]
    macs = rows * width * width * 6 + 4 * rows * rows * width
    res = pl.pallas_call(
        functools.partial(backward_kernel, pieces, rows, width),
        out_shape=[sds((chunk, width), BF16)] * pieces + [sds((8, width), F32)] + saved,
        in_specs=[SM] + [VM] * (2 * pieces) + [VM] * 2 + [ANY] * 9,
        out_specs=[VM] * (pieces + 1) + [ANY] * 4,
        scratch_shapes=[pltpu.VMEM(a.shape, a.dtype) for a in hbm_in[:8]] + [pltpu.VMEM((8, 128), F32)]
        + [pltpu.VMEM(s.shape, s.dtype) for s in saved]
        + [pltpu.VMEM((rows, width), BF16), pltpu.VMEM((rows, width), F32), pltpu.VMEM((8, width), F32)]
        + [pltpu.SemaphoreType.DMA((8,)), pltpu.SemaphoreType.DMA((4,))],
        compiler_params=pltpu.CompilerParams(vmem_limit_bytes=VMEM_LIMIT),
        cost_estimate=pl.CostEstimate(flops=2 * macs, bytes_accessed=32 << 20, transcendentals=0),
        name="slot_backward",
    )(share, *cots, *xs, *vecs, *hbm_in)
    return res[:pieces], res[pieces], res[pieces + 1:]


def weight_kernel(count, half, quarters, *refs):
    (spots,), refs = refs[:1], refs[1:]
    lefts, refs = refs[: 2 * count], refs[2 * count:]
    rights, refs = refs[: 2 * count], refs[2 * count:]
    (left_kept, left_sent, right_kept, right_sent, turned) = refs
    step = pl.program_id(0)
    per = pl.num_programs(0) // count
    rows, width = lefts[0].shape
    blocks = spots.shape[0]
    share = width // blocks
    for c in range(count):

        @pl.when(step == c * per)
        def _():
            for s in range(2):
                left = lefts[2 * c + s]
                for b in range(width // 128):
                    part = left[:, b * 128:(b + 1) * 128].T
                    for t in range(128 // share):
                        spot = pl.multiple_of(spots[b * (128 // share) + t] * share, share)
                        turned[pl.ds(spot, share), s * rows:(s + 1) * rows] = part[t * share:(t + 1) * share]

    def tile(right_a, right_b):
        return (dot(turned[:, :rows], right_a[...]) + dot(turned[:, rows:], right_b[...])).astype(BF16)

    quarter = width // 8

    def put(value):
        @pl.when(step < half)
        def _():
            left_kept[...] = value[: width // 2]
            left_sent[...] = value[width // 2:]

        @pl.when(step >= half)
        def _():
            for a, b in enumerate(quarters):
                right_kept[a * quarter:(a + 1) * quarter] = value[b * quarter:(b + 1) * quarter]
                right_sent[a * quarter:(a + 1) * quarter] = value[width // 2 + b * quarter:width // 2 + (b + 1) * quarter]

    if count == 1:
        put(tile(rights[0], rights[1]))
    else:
        for c in range(count):

            @pl.when(step // per == c)
            def _():
                put(tile(rights[2 * c], rights[2 * c + 1]))


def weight_grads(spots, quarters, lefts, rights, name):
    count = len(lefts)
    rows, width = lefts[0][0].shape
    columns = rights[0][0].shape[1] * count
    tile = 256
    steps = columns // tile
    per = steps // count
    half = steps // 2

    def right_spec(c):
        return pl.BlockSpec((rows, tile), lambda n, spots: (0, jnp.clip(n - c * per, 0, per - 1)))

    def out_spec(first):
        return pl.BlockSpec((width // 2, tile), lambda n, spots: (0, jnp.clip(n - first, 0, half - 1)))

    whole = pl.BlockSpec((rows, width), lambda n, spots: (0, 0))
    return pl.pallas_call(
        functools.partial(weight_kernel, count, half, quarters),
        out_shape=[jax.ShapeDtypeStruct((width // 2, columns // 2), BF16)] * 4,
        grid_spec=pltpu.PrefetchScalarGridSpec(
            num_scalar_prefetch=1,
            grid=(steps,),
            in_specs=[whole] * (2 * count) + [right_spec(c) for c in range(count) for _ in range(2)],
            out_specs=[out_spec(0), out_spec(0), out_spec(half), out_spec(half)],
            scratch_shapes=[pltpu.VMEM((width, 2 * rows), BF16)],
        ),
        compiler_params=pltpu.CompilerParams(vmem_limit_bytes=VMEM_LIMIT),
        cost_estimate=pl.CostEstimate(flops=4 * rows * width * columns, bytes_accessed=24 << 20, transcendentals=0),
        name=name,
    )(spots, *[a for pair in lefts for a in pair], *[a for pair in rights for a in pair])


def bits_of(extent):
    return [1 << i for i in range(extent.bit_length() - 1)]


def exchange(values, axis, bit):
    extent = lax.axis_size(axis)
    return lax.ppermute(values, axis, [(i, i ^ bit) for i in range(extent)])


def reduce_steps(kept, sent, order, share):
    columns = kept.shape[-1]
    kept = kept.reshape(-1, share, columns)
    sent = sent.reshape(-1, share, columns)
    for i, (axis, bit) in enumerate(order):
        total = kept.astype(F32) + exchange(sent, axis, bit).astype(F32)
        if i < len(order) - 1:
            middle = total.shape[0] // 2
            kept, sent = total[:middle], total[middle:].astype(BF16)
    return total[0]


def local(
    latents, cotangent, slot_crops, ln1_scale, ln1_offset, qkv_weight, out_weight, out_bias,
    ln2_scale, ln2_offset, up_weight, up_bias, down_weight, down_bias,
):
    slots, chunk, width = latents.shape
    images, lanes = lax.axis_size("img"), lax.axis_size("row")
    row = lax.axis_index("row")
    rounds = slots // lanes
    share = jnp.where(slot_crops > 0, 1.0 / jnp.maximum(slot_crops, 1).astype(F32), 0.0)

    def gather(values):
        blocks = values.reshape(rounds, lanes, chunk, width)
        got = []
        for k in range(lanes):
            mine = lax.dynamic_index_in_dim(blocks, row ^ k, 1, keepdims=False)
            got.append(mine if k == 0 else exchange(mine, "row", k))
        return got

    xs = gather(latents)
    cots = gather(cotangent)
    as_row = lambda v: v.reshape(1, -1)
    vecs = [as_row(v) for v in (ln1_scale, ln1_offset, ln2_scale, ln2_offset, out_bias, up_bias, down_bias)]
    mats = [qkv_weight, out_weight, up_weight, down_weight]
    saved, outs, grads, sums, wgs = [], [], [], [], []
    for r in range(rounds):
        full = lax.dynamic_slice(slot_crops, (r * lanes + row,), (1,))
        out, keep = forward(full, [x[r] for x in xs], vecs, mats)
        outs.append(out)
        saved.append(keep)
    for r in range(rounds):
        part = lax.dynamic_slice(share, (r * lanes + row,), (1,))
        h1, qkv, probs, mixed, resid, h2, pre, act = saved[r]
        grad, total, wg = backward(
            part, [c[r] for c in cots], [x[r] for x in xs], [vecs[0], vecs[2]],
            [down_weight, pre, up_weight, resid, out_weight, qkv, probs, qkv_weight, qkv_weight],
        )
        grads.append(grad)
        sums.append(total)
        wgs.append(wg)

    def scatter(pieces):
        back = []
        for k in range(lanes):
            mine = jnp.stack([pieces[r][k] for r in range(rounds)])
            back.append(mine if k == 0 else exchange(mine, "row", k))
        both = jnp.stack(back, 1)
        order = jnp.arange(lanes) ^ row
        return jnp.take(both, order, axis=1).reshape(slots, chunk, width)

    block_out = scatter(outs)
    latents_grad = scatter(grads)

    devices = images * lanes
    me = lax.axis_index("img") * lanes + row
    core, others = 1, bits_of(images)[1:]
    plan = [("img", core)] + [("img", b) for b in others] + [("row", b) for b in bits_of(lanes)]
    turned_plan = [("img", core)] + [("img", b) for b in reversed(others)] + [("row", b) for b in bits_of(lanes)]
    rows_of = width // devices
    relative = jnp.arange(devices, dtype=jnp.int32) ^ me

    def places(steps):
        spots = jnp.zeros_like(relative)
        for axis, bit in steps:
            spots = spots * 2 + (relative // (bit * lanes if axis == "img" else bit)) % 2
        return spots

    in_kernel = rows_of % 16 == 0 and len(others) == 2
    if in_kernel:
        spots, quarters = places(plan), (0, 2, 1, 3)
    else:
        spots, quarters = jnp.arange(width // 128, dtype=jnp.int32), (0, 1, 2, 3)
    pair = lambda index: [wgs[r][index] for r in range(rounds)]
    keep = lambda index: [saved[r][index] for r in range(rounds)]
    first = weight_grads(spots, quarters, [keep(7), keep(5), keep(3)], [pair(0), pair(1), pair(2)], "weights_first")
    second = weight_grads(spots, quarters, [keep(0)], [pair(3)], "weights_second")

    def arranged(kept, sent, steps):
        if in_kernel:
            return kept, sent
        natural = jnp.concatenate([kept, sent]).reshape(devices, rows_of, -1)
        placed = jnp.take(natural, jnp.argsort(places(steps)), axis=0)
        return placed[: devices // 2], placed[devices // 2:]

    def finish(parts):
        halves = []
        for kept, sent, steps in ((parts[0], parts[1], plan), (parts[2], parts[3], turned_plan)):
            halves.append(reduce_steps(*arranged(kept, sent, steps), steps, rows_of))
        return jnp.concatenate(halves, 1)

    mlp = finish(first)
    qkv_grad = finish(second)
    total = lax.psum_scatter(sum(sums), ("img", "row"), scatter_dimension=1, tiled=True)
    down_grad, up_grad, out_grad = jnp.split(mlp, 3, 1)
    return (
        block_out, latents_grad, total[5], total[6], qkv_grad, out_grad, total[4], total[2], total[3],
        up_grad, total[1], down_grad, total[0],
    )


def solution(mesh):
    whole, both = P(), P(("img", "row"))
    rows, wide = P("img", "row", None), P(("img", "row"), None)
    in_specs = (rows, rows, P("img")) + (whole,) * 11
    out_specs = (rows, rows, both, both, wide, wide, both, both, both, wide, both, wide, both)
    return jax.shard_map(local, mesh=mesh, in_specs=in_specs, out_specs=out_specs, check_vma=False)
```

```python
import functools
import jax
import jax.numpy as jnp
from jax import lax
from jax.experimental import pallas as pl
from jax.experimental.pallas import tpu as pltpu
from jax.sharding import PartitionSpec as P

HEADS = 8
EPSILON = 1e-05
F32 = jnp.float32
BF16 = jnp.bfloat16
MESH = pl.DeviceIdType.MESH
ANY = pl.BlockSpec(memory_space=pl.ANY)
VM = pl.BlockSpec(memory_space=pltpu.VMEM)
SM = pl.BlockSpec(memory_space=pltpu.SMEM)
GELU_A = 0.7978845608028654
GELU_B = 0.044715
LOG2_E = 1.4426950408889634
VMEM_LIMIT = 64 * 1024 * 1024 - 64 * 1024


def dot(a, b):
    return jnp.dot(a, b, preferred_element_type=F32)


def dot_t(a, b):
    return lax.dot_general(a, b, (((1,), (1,)), ((), ())), preferred_element_type=F32)


def dot_tt(a, b):
    return lax.dot_general(a, b, (((0,), (0,)), ((), ())), preferred_element_type=F32)


def norm_parts(values):
    mean = jnp.mean(values, -1, keepdims=True)
    centred = values - mean
    inverse = lax.rsqrt(jnp.mean(centred * centred, -1, keepdims=True) + EPSILON)
    return centred * inverse, inverse


def norm_back(scaled, hat, inverse):
    return inverse * (scaled - jnp.mean(scaled, -1, keepdims=True) - hat * jnp.mean(scaled * hat, -1, keepdims=True))


def column_sum(values):
    return jnp.sum(values, 0, keepdims=True)


def bits_of(extent):
    return [1 << i for i in range(extent.bit_length() - 1)]


def flipped(index, bit):
    return index + bit - 2 * bit * ((index // bit) % 2)


def block_kernel(images, lanes, rounds, steps_left, steps_right, *refs):
    (share_ref, keep_ref, lat, cot), refs = refs[:4], refs[4:]
    (scale1, offset1, scale2, offset2, bias_o, bias_u, bias_d), refs = refs[:7], refs[7:]
    mats, refs = refs[:4], refs[4:]
    (out_block, out_grad, mlp_out, qkv_out, sums_out), refs = refs[:5], refs[5:]
    (vq, vo, vu, vd, xr, cr, h1, qkv, resid, work, gl, gp, ga, gm, bo, lse, sums, sums_got, got_first, got_next), refs = refs[:20], refs[20:]
    (mat_sem, own_sem, lat_out, lat_in, cot_out, cot_in, bo_out, bo_in, lg_out, lg_in,
     red_out, red_in, credit, sum_out, sum_in) = refs
    rows, width = h1.shape[1:]
    chunk = rows // lanes
    size = width // HEADS
    img, z = lax.axis_index("img"), lax.axis_index("row")
    slope, act, h2, mixed = ([2 * i, 2 * i + 1] for i in (0, 4, 3, 5))

    def device(axis, bit):
        return (flipped(img, bit), z) if axis == "img" else (img, flipped(z, bit))

    def lane(k):
        other = z
        for bit in bits_of(lanes):
            if k & bit:
                other = flipped(other, bit)
        return other

    partners = {(axis, bit) for axis, bit in steps_left} | {("row", bit) for bit in bits_of(lanes)}
    friends = [device(axis, bit) for axis, bit in sorted(partners)]
    friends += [(img, lane(k)) for k in range(1, lanes) if k & (k - 1)]
    barrier = pltpu.get_barrier_semaphore()
    for friend in friends:
        pl.semaphore_signal(barrier, inc=1, device_id=friend, device_id_type=MESH)
    loads = [pltpu.make_async_copy(a, b, mat_sem.at[i]) for i, (a, b) in enumerate(zip(mats, (vq, vo, vu, vd)))]

    def pieces_in(source, target, sent, got, own):
        moves = []
        for r in range(rounds):
            moves.append([pltpu.make_async_copy(source.at[r * lanes + z], target.at[r, pl.ds(0, chunk)], own_sem.at[own, r])])
            for k in range(1, lanes):
                moves[r].append(pltpu.make_async_remote_copy(
                    src_ref=source.at[r * lanes + lane(k)], dst_ref=target.at[r, pl.ds(k * chunk, chunk)],
                    send_sem=sent.at[r, k], recv_sem=got.at[r, k], device_id=(img, lane(k)), device_id_type=MESH))
        return moves

    def pieces_out(source, target, sent, got, own):
        moves = []
        for r in range(rounds):
            moves.append([pltpu.make_async_copy(source.at[r, pl.ds(0, chunk)], target.at[r * lanes + z], own_sem.at[own, r])])
            for k in range(1, lanes):
                moves[r].append(pltpu.make_async_remote_copy(
                    src_ref=source.at[r, pl.ds(k * chunk, chunk)], dst_ref=target.at[r * lanes + z],
                    send_sem=sent.at[r, k], recv_sem=got.at[r, k], device_id=(img, lane(k)), device_id_type=MESH))
        return moves

    lat_moves = pieces_in(lat, xr, lat_out, lat_in, 0)
    cot_moves = pieces_in(cot, cr, cot_out, cot_in, 1)
    bo_moves = pieces_out(bo, out_block, bo_out, bo_in, 2)
    lg_moves = pieces_out(xr, out_grad, lg_out, lg_in, 3)

    def arrive(moves, k):
        moves[0].wait() if k == 0 else moves[k].wait_recv()

    for load in loads:
        load.start()
    for moves in (lat_moves, cot_moves):
        for r in range(rounds):
            moves[r][0].start()
    pl.semaphore_wait(barrier, len(friends))
    for moves in (lat_moves, cot_moves):
        for r in range(rounds):
            for move in moves[r][1:]:
                move.start()

    def halves():
        half = 2 * chunk if lanes % 2 == 0 else rows
        return [pl.ds(i * half, half) for i in range(rows // half)]

    def forward(r):
        s1, o1 = scale1[...].astype(F32), offset1[...].astype(F32)
        for k in range(lanes):
            arrive(lat_moves[r], k)
            part = pl.ds(k * chunk, chunk)
            hat, _ = norm_parts(xr[r, part, :].astype(F32))
            h1[r, part, :] = (hat * s1 + o1).astype(BF16)
        if r == 0:
            loads[0].wait()
        for n in range(3):
            qkv[3 * r + n] = dot(h1[r], vq[:, n * width:(n + 1) * width]).astype(BF16)
        factor = size ** -0.5 * LOG2_E
        for h in range(HEADS):
            cols = slice(h * size, (h + 1) * size)
            q, k, v = qkv[3 * r, :, cols], qkv[3 * r + 1, :, cols], qkv[3 * r + 2, :, cols]
            s = dot_t(q, k)
            top = jnp.max(s, 1, keepdims=True)
            e = jnp.exp2((s - top) * factor)
            total = jnp.sum(e, 1, keepdims=True)
            lse[r, :, h:h + 1] = top * factor + jnp.log2(total)
            work[mixed[r], :, cols] = (dot(e.astype(BF16), v) * (1.0 / total)).astype(BF16)
        if r == 0:
            loads[1].wait()
        bo_ = bias_o[...].astype(F32)
        s2, o2 = scale2[...].astype(F32), offset2[...].astype(F32)
        for part in halves():
            value = xr[r, part, :].astype(F32) + dot(work[mixed[r], part, :], vo[...]) + bo_
            resid[r, part, :] = value
            hat, _ = norm_parts(value)
            work[h2[r], part, :] = (hat * s2 + o2).astype(BF16)
        if r == 0:
            loads[2].wait()
        bu = bias_u[...].astype(F32)
        for part in halves():
            u = dot(work[h2[r], part, :], vu[...]) + bu
            t = jnp.tanh(GELU_A * (u + GELU_B * u * u * u))
            work[act[r], part, :] = (0.5 * u * (1.0 + t)).astype(BF16)
            work[slope[r], part, :] = (
                0.5 * (1.0 + t) + 0.5 * u * (1.0 - t * t) * (GELU_A * (1.0 + 3.0 * GELU_B * u * u))
            ).astype(BF16)
        if r == 0:
            loads[3].wait()
        bd = bias_d[...].astype(F32)
        keep = keep_ref[r * lanes + z]
        for part in halves():
            value = resid[r, part, :] + dot(work[act[r], part, :], vd[...]) + bd
            bo[r, part, :] = (value * keep).astype(BF16)
        for move in bo_moves[r]:
            move.start()

    def add_sum(index, value):
        sums[0, index:index + 1, :] = sums[0, index:index + 1, :] + value

    def backward_mlp(r):
        part_share = share_ref[r * lanes + z]
        for k in range(lanes):
            arrive(cot_moves[r], k)
            part = pl.ds(k * chunk, chunk)
            g = (cr[r, part, :].astype(F32) * part_share).astype(BF16)
            gl[r, part, :] = g
            add_sum(0, column_sum(g.astype(F32)))
        for part in halves():
            g = (dot_t(gl[r, part, :], vd[...]) * work[slope[r], part, :].astype(F32)).astype(BF16)
            gp[r, part, :] = g
            add_sum(1, column_sum(g.astype(F32)))
        s2 = scale2[...].astype(F32)
        for part in halves():
            gh = dot_t(gp[r, part, :], vu[...])
            hat, inverse = norm_parts(resid[r, part, :])
            add_sum(2, column_sum(gh * hat))
            add_sum(3, column_sum(gh))
            value = cr[r, part, :].astype(F32) * part_share + norm_back(gh * s2, hat, inverse)
            resid[r, part, :] = value
            g = value.astype(BF16)
            ga[r, part, :] = g
            add_sum(4, column_sum(g.astype(F32)))
        for part in halves():
            gm[r, part, :] = dot_t(ga[r, part, :], vo[...]).astype(BF16)

    def backward_attention(r):
        factor = size ** -0.5
        rows_of_lse = lse[r].T
        for h in range(HEADS):
            cols = slice(h * size, (h + 1) * size)
            q, k, v, m = qkv[3 * r, :, cols], qkv[3 * r + 1, :, cols], qkv[3 * r + 2, :, cols], gm[r, :, cols]
            p = jnp.exp2(dot_t(k, q) * (factor * LOG2_E) - rows_of_lse[h:h + 1, :])
            dp = dot_t(v, m)
            ds = (p * (dp - jnp.sum(p * dp, 0, keepdims=True))).astype(BF16)
            qkv[3 * r + 2, :, cols] = dot(p.astype(BF16), m).astype(BF16)
            qkv[3 * r + 1, :, cols] = (dot(ds, q) * factor).astype(BF16)
            qkv[3 * r, :, cols] = (dot(k.T, ds) * factor).T.astype(BF16)

    def backward_input(r):
        s1 = scale1[...].astype(F32)
        for part in halves():
            gh = dot_t(qkv[3 * r, part, :], vq[:, :width])
            gh = gh + dot_t(qkv[3 * r + 1, part, :], vq[:, width:2 * width])
            gh = gh + dot_t(qkv[3 * r + 2, part, :], vq[:, 2 * width:])
            hat, inverse = norm_parts(xr[r, part, :].astype(F32))
            add_sum(5, column_sum(gh * hat))
            add_sum(6, column_sum(gh))
            xr[r, part, :] = (resid[r, part, :] + norm_back(gh * s1, hat, inverse)).astype(BF16)
        for move in lg_moves[r]:
            move.start()

    count = len(steps_left)
    unit = width >> count
    per_half = width // 2 // unit
    sides = (slice(0, width // 2), slice(width // 2, width))

    def spot(block, steps):
        place = 0
        for axis, bit in steps:
            mine = (img // bit) % 2 if axis == "img" else (z // bit) % 2
            scale = 1 if axis == "row" else (width // unit) // images
            theirs = (block // (bit * scale)) % 2
            place = place * 2 + (theirs + mine) % 2
        return place

    def place_products(base, c, left, right):
        for cols, steps in zip(sides, (steps_left, steps_right)):
            total = dot_tt(left(0), right(0)[:, cols])
            for r in range(1, rounds):
                total = total + dot_tt(left(r), right(r)[:, cols])
            total = total.astype(BF16)
            for block in range(width // unit):
                at = spot(block, steps)
                page = base + c + 3 * (at // per_half)
                first = pl.multiple_of((at % per_half) * unit, unit)
                work[page, pl.ds(first, unit), cols] = total[block * unit:(block + 1) * unit]

    def send(base, group, step, side):
        steps = (steps_left, steps_right)[side]
        if step == 0:
            source, target = work.at[pl.ds(base + 3, 3)], got_first
        else:
            length = rows >> step
            source = work.at[pl.ds(base, 3), pl.ds(length, length), sides[side]]
            target = got_next.at[:, pl.ds(rows - 2 * length, length), sides[side]]
        return pltpu.make_async_remote_copy(
            src_ref=source, dst_ref=target, send_sem=red_out.at[group, step, side], recv_sem=red_in.at[group, step, side],
            device_id=device(*steps[step]), device_id_type=MESH)

    def begin(base, group, step, side):
        if group:
            pl.semaphore_wait(credit.at[step, side], 1)
        send(base, group, step, side).start()

    def reduce_step(base, group, step):
        for side in (0, 1):
            cols = sides[side]
            if step == 0 and side == 0:
                send(base, group, 0, 0).wait_recv()
            elif step:
                send(base, group, step, side).wait_recv()
            length = rows >> step
            half = length // 2

            def added(first, extent):
                part = pl.ds(first, extent)
                if step == 0:
                    got = got_first[:, part, cols]
                else:
                    got = got_next[:, pl.ds(rows - 2 * length + first, extent), cols]
                return work[pl.ds(base, 3), part, cols].astype(F32) + got.astype(F32)

            if step == count - 1:
                target = (mlp_out, qkv_out)[group]
                target[:, :, cols] = added(0, length)
            else:
                work[pl.ds(base, 3), pl.ds(half, half), cols] = added(half, half).astype(BF16)
                begin(base, group, step + 1, side)
                work[pl.ds(base, 3), pl.ds(0, half), cols] = added(0, half).astype(BF16)
            if group == 0 and (step or side):
                steps = (steps_left, steps_right)[side]
                pl.semaphore_signal(
                    credit.at[step, side if step else 0], inc=1, device_id=device(*steps[step]), device_id_type=MESH)

    sums[...] = jnp.zeros_like(sums)
    for r in range(rounds):
        forward(r)
    backward_mlp(0)
    backward_attention(0)
    backward_input(0)
    backward_mlp(1)
    place_products(0, 0, lambda r: work[act[r]], lambda r: gl[r])
    place_products(0, 1, lambda r: work[h2[r]], lambda r: gp[r])
    place_products(0, 2, lambda r: work[mixed[r]], lambda r: ga[r])
    begin(0, 0, 0, 0)
    backward_attention(1)
    reduce_step(0, 0, 0)
    for n in range(3):
        place_products(6, n, lambda r: h1[r], lambda r: qkv[3 * r + n])
    begin(6, 1, 0, 0)
    backward_input(1)
    sum_moves = [
        pltpu.make_async_remote_copy(
            src_ref=sums.at[i], dst_ref=sums_got.at[i], send_sem=sum_out.at[i], recv_sem=sum_in.at[i],
            device_id=device(axis, bit), device_id_type=MESH)
        for i, (axis, bit) in enumerate(steps_left)
    ]
    sum_moves[0].start()
    for step in range(1, count + 1):
        if step < count:
            reduce_step(0, 0, step)
        reduce_step(6, 1, step - 1)
        sum_moves[step - 1].wait()
        sums[step] = sums[step - 1] + sums_got[step - 1]
        if step < count:
            sum_moves[step].start()
    sums_out[...] = sums[count]

    for group, base in enumerate((0, 6)):
        send(base, group, 0, 0).wait_send()
        for step in range(1, count):
            for side in (0, 1):
                send(base, group, step, side).wait_send()
    for r in range(rounds):
        for k in range(1, lanes):
            lat_moves[r][k].wait_send()
            cot_moves[r][k].wait_send()
        for moves in (bo_moves, lg_moves):
            for move in moves[r]:
                move.wait()


def local(
    latents, cotangent, slot_crops, ln1_scale, ln1_offset, qkv_weight, out_weight, out_bias,
    ln2_scale, ln2_offset, up_weight, up_bias, down_weight, down_bias,
):
    slots, chunk, width = latents.shape
    images, lanes = lax.axis_size("img"), lax.axis_size("row")
    rounds = slots // lanes
    rows = chunk * lanes
    devices = images * lanes
    valid = slot_crops > 0
    share = jnp.where(valid, 1.0 / jnp.maximum(slot_crops, 1).astype(F32), 0.0)
    image_bits = bits_of(images)
    left = [("img", image_bits[0])] + [("img", b) for b in image_bits[1:]]
    right = [("img", image_bits[0])] + [("img", b) for b in reversed(image_bits[1:])]
    whole_sum = width // devices >= 16
    if whole_sum:
        lane_steps = [("row", b) for b in bits_of(lanes)]
        left, right = left + lane_steps, right + lane_steps
    count = len(left)
    unit = width >> count
    sds = jax.ShapeDtypeStruct
    as_row = lambda v: v.reshape(1, -1)
    vecs = [as_row(v) for v in (ln1_scale, ln1_offset, ln2_scale, ln2_offset, out_bias, up_bias, down_bias)]
    page = lambda n, kind=BF16: pltpu.VMEM((n, rows, width), kind)
    dma = lambda *shape: pltpu.SemaphoreType.DMA(shape)
    macs = rounds * (rows * width * width * 18 + rows * rows * width * 7)
    block_out, latents_grad, mlp, qkv_grad, totals = pl.pallas_call(
        functools.partial(block_kernel, images, lanes, rounds, left, right),
        out_shape=[sds(latents.shape, BF16)] * 2 + [sds((3, unit, width), F32)] * 2 + [sds((8, width), F32)],
        in_specs=[SM] * 2 + [ANY] * 2 + [VM] * 7 + [ANY] * 4,
        out_specs=[ANY] * 2 + [VM] * 3,
        scratch_shapes=[
            pltpu.VMEM((width, 3 * width), BF16), pltpu.VMEM((width, width), BF16), pltpu.VMEM((width, width), BF16),
            pltpu.VMEM((width, width), BF16),
            page(rounds), page(rounds), page(rounds), page(3 * rounds), page(rounds, F32), page(12),
            page(rounds), page(rounds), page(rounds), page(rounds), page(rounds),
            pltpu.VMEM((rounds, rows, 128), F32), pltpu.VMEM((count + 1, 8, width), F32), pltpu.VMEM((count, 8, width), F32),
            page(3), page(3),
            dma(4), dma(4, rounds),
            dma(rounds, lanes), dma(rounds, lanes), dma(rounds, lanes), dma(rounds, lanes),
            dma(rounds, lanes), dma(rounds, lanes), dma(rounds, lanes), dma(rounds, lanes),
            dma(2, count, 2), dma(2, count, 2), pltpu.SemaphoreType.REGULAR((count, 2)), dma(count), dma(count),
        ],
        compiler_params=pltpu.CompilerParams(collective_id=0, has_side_effects=True, vmem_limit_bytes=VMEM_LIMIT),
        cost_estimate=pl.CostEstimate(flops=2 * macs, bytes_accessed=32 << 20, transcendentals=0),
        name="latent_block",
    )(share, valid.astype(F32), latents, cotangent, *vecs, qkv_weight, out_weight, up_weight, down_weight)
    if not whole_sum:
        mlp = lax.psum_scatter(mlp, "row", scatter_dimension=1, tiled=True)
        qkv_grad = lax.psum_scatter(qkv_grad, "row", scatter_dimension=1, tiled=True)
        totals = lax.psum(totals, "row")
    me = lax.axis_index("img") * lanes + lax.axis_index("row")
    part = width // devices
    mine = lax.dynamic_slice(totals, (0, me * part), (8, part))
    return (
        block_out, latents_grad, mine[5], mine[6], jnp.concatenate([qkv_grad[0], qkv_grad[1], qkv_grad[2]], 1), mlp[2], mine[4],
        mine[2], mine[3], mlp[1], mine[1], mlp[0], mine[0],
    )


def solution(mesh):
    whole, both = P(), P(("img", "row"))
    rows, wide = P("img", "row", None), P(("img", "row"), None)
    in_specs = (rows, rows, P("img")) + (whole,) * 11
    out_specs = (rows, rows, both, both, wide, wide, both, both, both, wide, both, wide, both)
    return jax.shard_map(local, mesh=mesh, in_specs=in_specs, out_specs=out_specs, check_vma=False)
```

```python
import functools
import jax
import jax.numpy as jnp
from jax import lax
from jax.experimental import pallas as pl
from jax.experimental.pallas import tpu as pltpu
from jax.sharding import PartitionSpec as P

HEADS = 8
EPSILON = 1e-05
F32 = jnp.float32
BF16 = jnp.bfloat16
MESH = pl.DeviceIdType.MESH
ANY = pl.BlockSpec(memory_space=pl.ANY)
VM = pl.BlockSpec(memory_space=pltpu.VMEM)
SM = pl.BlockSpec(memory_space=pltpu.SMEM)
GELU_A = 0.7978845608028654
GELU_B = 0.044715
LOG2_E = 1.4426950408889634
VMEM_LIMIT = 64 * 1024 * 1024 - 64 * 1024


def dot(a, b):
    return jnp.dot(a, b, preferred_element_type=F32)


def dot_t(a, b):
    return lax.dot_general(a, b, (((1,), (1,)), ((), ())), preferred_element_type=F32)


def dot_tt(a, b):
    return lax.dot_general(a, b, (((0,), (0,)), ((), ())), preferred_element_type=F32)


def norm_parts(values):
    mean = jnp.mean(values, -1, keepdims=True)
    centred = values - mean
    inverse = lax.rsqrt(jnp.mean(centred * centred, -1, keepdims=True) + EPSILON)
    return centred * inverse, inverse


def norm_back(scaled, hat, inverse):
    return inverse * (scaled - jnp.mean(scaled, -1, keepdims=True) - hat * jnp.mean(scaled * hat, -1, keepdims=True))


def column_sum(values):
    return jnp.sum(values, 0, keepdims=True)


def bits_of(extent):
    return [1 << i for i in range(extent.bit_length() - 1)]


def flipped(index, bit):
    return index + bit - 2 * bit * ((index // bit) % 2)


def block_kernel(images, lanes, places, steps_left, steps_right, in_lanes, *refs):
    crops, vectors, (lat, cot), refs = refs[0], refs[1:8], refs[8:10], refs[10:]
    mats, refs = refs[:4], refs[4:]
    (out_block, out_grad), refs = refs[:2], refs[2:]
    mlp_out, (qkv_out, sums_out), refs = refs[:3], refs[3:5], refs[5:]
    (vq, vo, vu, vd, xr, cr, h1, qkv, resid, work, back, gm, bo, lse, sums, sums_got, got_first, got_next), refs = refs[:18], refs[18:]
    (mat_sem, own_sem, lat_out, lat_in, cot_out, cot_in, bo_out, bo_in, lg_out, lg_in,
     red_out, red_in, credit, sum_out, sum_in) = refs
    rounds, rows, width = h1.shape
    chunk = rows // lanes
    size = width // HEADS
    img, z = lax.axis_index("img"), lax.axis_index("row")
    left_pages, slope = 6, 0
    act, h2, mixed = (left_pages + rounds * i for i in range(3))
    gl, gp, ga = (rounds * i for i in range(3))
    last = rounds - 1

    def device(axis, bit):
        return (flipped(img, bit), z) if axis == "img" else (img, flipped(z, bit))

    def lane(k):
        other = z
        for bit in bits_of(lanes):
            if k & bit:
                other = flipped(other, bit)
        return other

    def place(r, other):
        return r * lanes + other

    def loop_rounds(body):
        pl.loop(0, rounds)(body)

    partners = {(axis, bit) for axis, bit in steps_left} | {("row", bit) for bit in bits_of(lanes)}
    friends = [device(axis, bit) for axis, bit in sorted(partners)]
    friends += [(img, lane(k)) for k in range(1, lanes) if k & (k - 1)]
    barrier = pltpu.get_barrier_semaphore()
    for friend in friends:
        pl.semaphore_signal(barrier, inc=1, device_id=friend, device_id_type=MESH)
    loads = [pltpu.make_async_copy(a, b, mat_sem.at[i]) for i, (a, b) in enumerate(zip(mats, (vq, vo, vu, vd)))]

    def piece_in(source, target, sent, got, own, r, k):
        if k == 0:
            return pltpu.make_async_copy(source.at[place(r, z)], target.at[r, pl.ds(0, chunk)], own_sem.at[own, r])
        return pltpu.make_async_remote_copy(
            src_ref=source.at[place(r, lane(k))], dst_ref=target.at[r, pl.ds(k * chunk, chunk)],
            send_sem=sent.at[r, k], recv_sem=got.at[r, k], device_id=(img, lane(k)), device_id_type=MESH)

    def piece_out(source, target, sent, got, own, r, k):
        if k == 0:
            return pltpu.make_async_copy(source.at[r, pl.ds(0, chunk)], target.at[place(r, z)], own_sem.at[own, r])
        return pltpu.make_async_remote_copy(
            src_ref=source.at[r, pl.ds(k * chunk, chunk)], dst_ref=target.at[place(r, z)],
            send_sem=sent.at[r, k], recv_sem=got.at[r, k], device_id=(img, lane(k)), device_id_type=MESH)

    lat_piece = functools.partial(piece_in, lat, xr, lat_out, lat_in, 0)
    cot_piece = functools.partial(piece_in, cot, cr, cot_out, cot_in, 1)
    bo_piece = functools.partial(piece_out, bo, out_block, bo_out, bo_in, 2)
    lg_piece = functools.partial(piece_out, xr, out_grad, lg_out, lg_in, 3)

    def arrive(piece, r, k):
        move = piece(r, k)
        move.wait() if k == 0 else move.wait_recv()

    for load in loads:
        load.start()
    for piece in (lat_piece, cot_piece):
        for r in range(rounds):
            piece(r, 0).start()
    sums[...] = jnp.zeros_like(sums)
    pl.semaphore_wait(barrier, len(friends))

    def issue(piece, r):
        for k in range(lanes - 1, 0, -1):
            piece(r, k).start()

    issue(lat_piece, 0)

    half = rows // 2
    halves = [pl.ds(i * half, half) for i in range(2)]
    vector = lambda i: vectors[i][...].astype(F32).reshape(1, width)

    def head_columns(h):
        return pl.ds(pl.multiple_of(h * size, size), size)

    def forward(r):
        s1, o1 = vector(0), vector(1)
        for k in range(lanes):
            arrive(lat_piece, r, k)
            part = pl.ds(k * chunk, chunk)
            hat, _ = norm_parts(xr[r, part, :].astype(F32))
            h1[r, part, :] = (hat * s1 + o1).astype(BF16)

        @pl.when(r < last)
        def _():
            issue(lat_piece, r + 1)

        @pl.when(r == last)
        def _():
            issue(cot_piece, 0)

        for n in range(3):
            qkv[3 * r + n] = dot(h1[r], vq[:, n * width:(n + 1) * width]).astype(BF16)
        factor = size ** -0.5 * LOG2_E

        @pl.loop(0, HEADS // 4)
        def _(group):
            for i in range(4):
                cols = head_columns(4 * group + i)
                q, k, v = qkv[3 * r, :, cols], qkv[3 * r + 1, :, cols], qkv[3 * r + 2, :, cols]
                s = dot_t(q, k)
                top = jnp.max(s, 1, keepdims=True)
                e = jnp.exp2((s - top) * factor)
                total = jnp.sum(e, 1, keepdims=True)
                lse[r, group, :, i:i + 1] = top * factor + jnp.log2(total)
                work[mixed + r, :, cols] = (dot(e.astype(BF16), v) * (1.0 / total)).astype(BF16)

        bo_, s2, o2 = vector(4), vector(2), vector(3)
        for part in halves:
            value = xr[r, part, :].astype(F32) + dot(work[mixed + r, part, :], vo[...]) + bo_
            resid[r, part, :] = value
            hat, _ = norm_parts(value)
            work[h2 + r, part, :] = (hat * s2 + o2).astype(BF16)
        bu = vector(5)
        for part in halves:
            u = dot(work[h2 + r, part, :], vu[...]) + bu
            t = jnp.tanh(GELU_A * (u + GELU_B * u * u * u))
            work[act + r, part, :] = (0.5 * u * (1.0 + t)).astype(BF16)
            work[slope + r, part, :] = (
                0.5 * (1.0 + t) + 0.5 * u * (1.0 - t * t) * (GELU_A * (1.0 + 3.0 * GELU_B * u * u))
            ).astype(BF16)
        bd = vector(6)
        keep = jnp.minimum(crops[place(r, z)], 1).astype(F32)
        for part in halves:
            value = resid[r, part, :] + dot(work[act + r, part, :], vd[...]) + bd
            bo[r, part, :] = (value * keep).astype(BF16)
        bo_piece(r, 0).start()

    def add_sum(index, value):
        sums[0, index:index + 1, :] = sums[0, index:index + 1, :] + value

    def backward_mlp(r):
        held = crops[place(r, z)]
        share = jnp.full((1, width), jnp.minimum(held, 1).astype(F32)) / jnp.full((1, width), jnp.maximum(held, 1).astype(F32))
        for k in range(lanes):
            arrive(cot_piece, r, k)
            part = pl.ds(k * chunk, chunk)
            g = (cr[r, part, :].astype(F32) * share).astype(BF16)
            back[gl + r, part, :] = g
            add_sum(0, column_sum(g.astype(F32)))

        @pl.when(r < last)
        def _():
            issue(cot_piece, r + 1)

        @pl.when(r == last)
        def _():
            for s in range(rounds):
                issue(bo_piece, s)

        for part in halves:
            g = (dot_t(back[gl + r, part, :], vd[...]) * work[slope + r, part, :].astype(F32)).astype(BF16)
            back[gp + r, part, :] = g
            add_sum(1, column_sum(g.astype(F32)))
        s2 = vector(2)
        for part in halves:
            gh = dot_t(back[gp + r, part, :], vu[...])
            hat, inverse = norm_parts(resid[r, part, :])
            add_sum(2, column_sum(gh * hat))
            add_sum(3, column_sum(gh))
            value = cr[r, part, :].astype(F32) * share + norm_back(gh * s2, hat, inverse)
            resid[r, part, :] = value
            g = value.astype(BF16)
            back[ga + r, part, :] = g
            add_sum(4, column_sum(g.astype(F32)))
        for part in halves:
            gm[0, part, :] = dot_t(back[ga + r, part, :], vo[...]).astype(BF16)

    def backward_attention(r):
        factor = size ** -0.5

        for h in range(HEADS):
            if h % 4 == 0:
                lse_rows = lse[r, h // 4].T
            cols = slice(h * size, (h + 1) * size)
            q, k, v, m = qkv[3 * r, :, cols], qkv[3 * r + 1, :, cols], qkv[3 * r + 2, :, cols], gm[0, :, cols]
            p = jnp.exp2(dot_t(k, q) * (factor * LOG2_E) - lse_rows[h % 4:h % 4 + 1, :])
            dp = dot_t(v, m)
            ds = (p * (dp - jnp.sum(p * dp, 0, keepdims=True))).astype(BF16)
            qkv[3 * r + 2, :, cols] = dot(p.astype(BF16), m).astype(BF16)
            qkv[3 * r + 1, :, cols] = (dot(ds, q) * factor).astype(BF16)
            qkv[3 * r, :, cols] = (dot(k.T, ds) * factor).T.astype(BF16)

    def backward_input(r):
        s1 = vector(0)
        for part in halves:
            gh = dot_t(qkv[3 * r, part, :], vq[:, :width])
            gh = gh + dot_t(qkv[3 * r + 1, part, :], vq[:, width:2 * width])
            gh = gh + dot_t(qkv[3 * r + 2, part, :], vq[:, 2 * width:])
            hat, inverse = norm_parts(xr[r, part, :].astype(F32))
            add_sum(5, column_sum(gh * hat))
            add_sum(6, column_sum(gh))
            xr[r, part, :] = (resid[r, part, :] + norm_back(gh * s1, hat, inverse)).astype(BF16)

    count = len(steps_left)
    unit = width >> count
    per_half = width // 2 // unit
    sides = (slice(0, width // 2), slice(width // 2, width))

    def spot(block, steps):
        found = 0
        for axis, bit in steps:
            mine = (img // bit) % 2 if axis == "img" else (z // bit) % 2
            scale = 1 if axis == "row" else (width // unit) // images
            theirs = (block // (bit * scale)) % 2
            found = found * 2 + (theirs + mine) % 2
        return found

    def place_products(base, left, right):
        @pl.loop(0, 3)
        def _(c):
            for steps, offset in ((steps_left, 0), (steps_right, width // 2)):
                for first_column in range(offset, offset + width // 2, 256):
                    cols = slice(first_column, first_column + 256)
                    total = dot_tt(left(c, 0), right(c, 0, cols))
                    for r in range(1, rounds):
                        total = total + dot_tt(left(c, r), right(c, r, cols))
                    total = total.astype(BF16)
                    for block in range(width // unit):
                        at = spot(block, steps)
                        first = pl.multiple_of((at % per_half) * unit, unit)
                        work[base + c + 3 * (at // per_half), pl.ds(first, unit), cols] = total[block * unit:(block + 1) * unit]

    def send(base, group, step, side):
        steps = (steps_left, steps_right)[side]
        if step == 0:
            source, target = work.at[pl.ds(base + 3, 3)], got_first
        else:
            length = rows >> step
            source = work.at[pl.ds(base, 3), pl.ds(length, length), sides[side]]
            target = got_next.at[:, pl.ds(rows - 2 * length, length), sides[side]]
        return pltpu.make_async_remote_copy(
            src_ref=source, dst_ref=target, send_sem=red_out.at[group, step, side], recv_sem=red_in.at[group, step, side],
            device_id=device(*steps[step]), device_id_type=MESH)

    def begin(base, group, step, side):
        if group:
            pl.semaphore_wait(credit.at[step, side], 1)
        send(base, group, step, side).start()

    def reduce_step(base, group, step):
        length = rows >> step
        middle = length // 2
        for side in (0, 1):
            cols = sides[side]
            if step or side == 0:
                send(base, group, step, side).wait_recv()

            def added(c, first, extent):
                if step == 0:
                    got = got_first[c, pl.ds(first, extent), cols]
                else:
                    got = got_next[c, pl.ds(rows - 2 * length + first, extent), cols]
                return work[base + c, pl.ds(first, extent), cols].astype(F32) + got.astype(F32)

            if step == count - 1:
                for c in range(3):
                    if group:
                        qkv_out[:, c * width + cols.start:c * width + cols.stop] = added(c, 0, length)
                    else:
                        mlp_out[c][:, cols] = added(c, 0, length)
            else:
                def keep_part(first):
                    @pl.loop(0, 3)
                    def _(c):
                        work[base + c, pl.ds(first, middle), cols] = added(c, first, middle).astype(BF16)

                keep_part(middle)
                begin(base, group, step + 1, side)
                keep_part(0)
            if group == 0 and (step or side):
                steps = (steps_left, steps_right)[side]
                pl.semaphore_signal(
                    credit.at[step, side if step else 0], inc=1, device_id=device(*steps[step]), device_id_type=MESH)

    mlp_base, qkv_base = 0, left_pages
    for load in loads:
        load.wait()
    loop_rounds(forward)

    @loop_rounds
    def _(r):
        backward_mlp(r)

        @pl.when(r == last)
        def _():
            place_products(
                mlp_base, lambda c, s: work[left_pages + rounds * c + s], lambda c, s, cols: back[rounds * c + s, :, cols])
            begin(mlp_base, 0, 0, 0)

        backward_attention(r)

        @pl.when(r == last)
        def _():
            for s in range(last):
                issue(lg_piece, s)
            reduce_step(mlp_base, 0, 0)
            place_products(qkv_base, lambda c, s: h1[s], lambda c, s, cols: qkv[3 * s + c, :, cols])
            begin(qkv_base, 1, 0, 0)

        backward_input(r)
        lg_piece(r, 0).start()


    gates = {count - 3: [2], count - 2: [3], count - 1: [1]} if in_lanes and lanes == 4 else {0: range(1, lanes)}

    def results_out(step):
        for k in gates.get(step, ()):
            lg_piece(last, k).start()

    sum_moves = [
        pltpu.make_async_remote_copy(
            src_ref=sums.at[i], dst_ref=sums_got.at[i], send_sem=sum_out.at[i], recv_sem=sum_in.at[i],
            device_id=device(axis, bit), device_id_type=MESH)
        for i, (axis, bit) in enumerate(steps_left)
    ]
    sum_moves[0].start()
    results_out(0)
    for step in range(1, count + 1):
        if step < count:
            reduce_step(mlp_base, 0, step)
        if step == count - 3:
            results_out(step)
        reduce_step(qkv_base, 1, step - 1)
        if step > count - 3:
            results_out(step)
        sum_moves[step - 1].wait()
        sums[step] = sums[step - 1] + sums_got[step - 1]
        if step < count:
            sum_moves[step].start()
    sums_out[...] = sums[count]

    for group, base in enumerate((mlp_base, qkv_base)):
        send(base, group, 0, 0).wait_send()
        for step in range(1, count):
            for side in (0, 1):
                send(base, group, step, side).wait_send()
    for r in range(rounds):
        for k in range(1, lanes):
            lat_piece(r, k).wait_send()
            cot_piece(r, k).wait_send()
        for piece in (bo_piece, lg_piece):
            for k in range(lanes):
                piece(r, k).wait()


def local(
    latents, cotangent, slot_crops, ln1_scale, ln1_offset, qkv_weight, out_weight, out_bias,
    ln2_scale, ln2_offset, up_weight, up_bias, down_weight, down_bias,
):
    slots, chunk, width = latents.shape
    images, lanes = lax.axis_size("img"), lax.axis_size("row")
    rounds = slots // lanes
    rows = chunk * lanes
    devices = images * lanes
    image_bits = bits_of(images)
    left = [("img", image_bits[0])] + [("img", b) for b in image_bits[1:]]
    right = [("img", image_bits[0])] + [("img", b) for b in reversed(image_bits[1:])]
    whole_sum = width // devices >= 16
    if whole_sum:
        lane_steps = [("row", b) for b in bits_of(lanes)]
        left, right = left + lane_steps, right + lane_steps
    count = len(left)
    unit = width >> count
    sds = jax.ShapeDtypeStruct
    page = lambda n, kind=BF16: pltpu.VMEM((n, rows, width), kind)
    dma = lambda *shape: pltpu.SemaphoreType.DMA(shape)
    macs = rounds * (rows * width * width * 18 + rows * rows * width * 7)
    block_out, latents_grad, down_grad, up_grad, out_grad, qkv_grad, totals = pl.pallas_call(
        functools.partial(block_kernel, images, lanes, slots, left, right, whole_sum),
        out_shape=[sds(latents.shape, BF16)] * 2 + [sds((unit, width), F32)] * 3 + [sds((unit, 3 * width), F32), sds((8, width), F32)],
        in_specs=[SM] + [VM] * 7 + [ANY] * 6,
        out_specs=[ANY] * 2 + [VM] * 5,
        scratch_shapes=[
            pltpu.VMEM((width, 3 * width), BF16), pltpu.VMEM((width, width), BF16), pltpu.VMEM((width, width), BF16),
            pltpu.VMEM((width, width), BF16),
            page(rounds), page(rounds), page(rounds), page(3 * rounds), page(rounds, F32), page(6 + 3 * rounds),
            page(3 * rounds), page(1), page(rounds),
            pltpu.VMEM((rounds, HEADS // 4, rows, 128), F32),
            pltpu.VMEM((count + 1, 8, width), F32), pltpu.VMEM((count, 8, width), F32),
            page(3), page(3),
            dma(4), dma(4, rounds),
            dma(rounds, lanes), dma(rounds, lanes), dma(rounds, lanes), dma(rounds, lanes),
            dma(rounds, lanes), dma(rounds, lanes), dma(rounds, lanes), dma(rounds, lanes),
            dma(2, count, 2), dma(2, count, 2), pltpu.SemaphoreType.REGULAR((count, 2)), dma(count), dma(count),
        ],
        compiler_params=pltpu.CompilerParams(collective_id=0, has_side_effects=True, vmem_limit_bytes=VMEM_LIMIT),
        cost_estimate=pl.CostEstimate(flops=2 * macs, bytes_accessed=32 << 20, transcendentals=0),
        name="latent_block",
    )(slot_crops, ln1_scale, ln1_offset, ln2_scale, ln2_offset, out_bias, up_bias, down_bias, latents, cotangent, qkv_weight, out_weight, up_weight, down_weight)
    if not whole_sum:
        down_grad, up_grad, out_grad, qkv_grad = [
            lax.psum_scatter(g, "row", scatter_dimension=0, tiled=True) for g in (down_grad, up_grad, out_grad, qkv_grad)]
        totals = lax.psum(totals, "row")
    me = lax.axis_index("img") * lanes + lax.axis_index("row")
    part = width // devices
    mine = lax.dynamic_slice(totals, (0, me * part), (8, part))
    return (
        block_out, latents_grad, mine[5], mine[6], qkv_grad, out_grad, mine[4], mine[2], mine[3], up_grad, mine[1], down_grad,
        mine[0],
    )


def solution(mesh):
    whole, both = P(), P(("img", "row"))
    rows, wide = P("img", "row", None), P(("img", "row"), None)
    in_specs = (rows, rows, P("img")) + (whole,) * 11
    out_specs = (rows, rows, both, both, wide, wide, both, both, both, wide, both, wide, both)
    return jax.shard_map(local, mesh=mesh, in_specs=in_specs, out_specs=out_specs, check_vma=False)
```

```python
import functools
import jax
import jax.numpy as jnp
from jax import lax
from jax.experimental import pallas as pl
from jax.experimental.pallas import tpu as pltpu
from jax.sharding import PartitionSpec as P

HEADS = 8
EPSILON = 1e-05
F32 = jnp.float32
BF16 = jnp.bfloat16
MESH = pl.DeviceIdType.MESH
ANY = pl.BlockSpec(memory_space=pl.ANY)
VM = pl.BlockSpec(memory_space=pltpu.VMEM)
SM = pl.BlockSpec(memory_space=pltpu.SMEM)
GELU_A = 0.7978845608028654
GELU_B = 0.044715
LOG2_E = 1.4426950408889634
EARLY = {1: (3, 2), 3: (1,)}
VMEM_LIMIT = 64 * 1024 * 1024 - 64 * 1024


def dot(a, b):
    return jnp.dot(a, b, preferred_element_type=F32)


def dot_t(a, b):
    return lax.dot_general(a, b, (((1,), (1,)), ((), ())), preferred_element_type=F32)


def dot_tt(a, b):
    return lax.dot_general(a, b, (((0,), (0,)), ((), ())), preferred_element_type=F32)


def norm_parts(values):
    mean = jnp.mean(values, -1, keepdims=True)
    centred = values - mean
    inverse = lax.rsqrt(jnp.mean(centred * centred, -1, keepdims=True) + EPSILON)
    return centred * inverse, inverse


def norm_back(scaled, hat, inverse):
    return inverse * (scaled - jnp.mean(scaled, -1, keepdims=True) - hat * jnp.mean(scaled * hat, -1, keepdims=True))


def column_sum(values):
    return jnp.sum(values, 0, keepdims=True)


def bits_of(extent):
    return [1 << i for i in range(extent.bit_length() - 1)]


def flipped(index, bit):
    return index + bit - 2 * bit * ((index // bit) % 2)


def block_kernel(images, lanes, places, steps_left, steps_right, in_lanes, *refs):
    crops, vectors, (lat, cot), refs = refs[0], refs[1:8], refs[8:10], refs[10:]
    mats, refs = refs[:4], refs[4:]
    (results, products_out, sums_out), refs = refs[:3], refs[3:]
    (vq, vo, vu, vd, xr, cr, h1, qkv, resid, summed, factors, back, gm, bo, lse, sums, sums_got, got_first, got_next), refs = refs[:19], refs[19:]
    (mat_sem, own_sem, lat_out, lat_in, cot_out, cot_in, bo_out, bo_in, lg_out, lg_in,
     red_out, red_in, credit, sum_out, sum_in) = refs
    rounds, rows, width = h1.shape
    chunk = rows // lanes
    size = width // HEADS
    img, z = lax.axis_index("img"), lax.axis_index("row")
    act, h2, mixed = (rounds * i for i in range(3))
    gl, gp, ga = (rounds * i for i in range(3))
    last = rounds - 1

    def device(axis, bit):
        return (flipped(img, bit), z) if axis == "img" else (img, flipped(z, bit))

    def lane(k):
        other = z
        for bit in bits_of(lanes):
            if k & bit:
                other = flipped(other, bit)
        return other

    def place(r, other):
        return r * lanes + other

    def loop_rounds(body):
        pl.loop(0, rounds)(body)

    partners = {(axis, bit) for axis, bit in steps_left} | {("row", bit) for bit in bits_of(lanes)}
    friends = [device(axis, bit) for axis, bit in sorted(partners)]
    friends += [(img, lane(k)) for k in range(1, lanes) if k & (k - 1)]
    barrier = pltpu.get_barrier_semaphore()
    for friend in friends:
        pl.semaphore_signal(barrier, inc=1, device_id=friend, device_id_type=MESH)
    loads = [pltpu.make_async_copy(a, b, mat_sem.at[i]) for i, (a, b) in enumerate(zip(mats, (vq, vo, vu, vd)))]

    def piece_in(source, target, sent, got, own, r, k):
        if k == 0:
            return pltpu.make_async_copy(source.at[place(r, z)], target.at[r, pl.ds(0, chunk)], own_sem.at[own, r])
        return pltpu.make_async_remote_copy(
            src_ref=source.at[place(r, lane(k))], dst_ref=target.at[r, pl.ds(k * chunk, chunk)],
            send_sem=sent.at[r, k], recv_sem=got.at[r, k], device_id=(img, lane(k)), device_id_type=MESH)

    def piece_out(source, first, sent, got, own, r, k):
        target = results.at[first + place(r, z)]
        if k == 0:
            return pltpu.make_async_copy(source.at[r, pl.ds(0, chunk)], target, own_sem.at[own, r])
        return pltpu.make_async_remote_copy(
            src_ref=source.at[r, pl.ds(k * chunk, chunk)], dst_ref=target,
            send_sem=sent.at[r, k], recv_sem=got.at[r, k], device_id=(img, lane(k)), device_id_type=MESH)

    lat_piece = functools.partial(piece_in, lat, xr, lat_out, lat_in, 0)
    cot_piece = functools.partial(piece_in, cot, cr, cot_out, cot_in, 1)
    bo_piece = functools.partial(piece_out, bo, 0, bo_out, bo_in, 2)
    lg_piece = functools.partial(piece_out, xr, places, lg_out, lg_in, 3)

    def arrive(piece, r, k):
        move = piece(r, k)
        move.wait() if k == 0 else move.wait_recv()

    for load in loads:
        load.start()
    for piece in (lat_piece, cot_piece):
        for r in range(rounds):
            piece(r, 0).start()
    sums[...] = jnp.zeros_like(sums)
    pl.semaphore_wait(barrier, len(friends))

    def issue(piece, r):
        for k in range(lanes - 1, 0, -1):
            piece(r, k).start()

    issue(lat_piece, 0)

    def issue_next(piece, r, k):
        for kk in EARLY.get(k, ()):
            @pl.when(r < last)
            def _():
                piece(r + 1, kk).start()

            @pl.when(r == last)
            def _():
                if piece is lat_piece:
                    cot_piece(0, kk).start()
                else:
                    bo_piece(0, kk).start()

    half = rows // 2
    halves = [pl.ds(i * half, half) for i in range(2)]
    vector = lambda i: vectors[i][...].astype(F32).reshape(1, width)

    def head_columns(h):
        return pl.ds(pl.multiple_of(h * size, size), size)

    def forward(r):
        s1, o1 = vector(0), vector(1)
        for k in range(lanes):
            arrive(lat_piece, r, k)
            part = pl.ds(k * chunk, chunk)
            hat, _ = norm_parts(xr[r, part, :].astype(F32))
            h1[r, part, :] = (hat * s1 + o1).astype(BF16)
            issue_next(lat_piece, r, k)

        for n in range(3):
            qkv[3 * r + n] = dot(h1[r], vq[:, n * width:(n + 1) * width]).astype(BF16)
        factor = size ** -0.5 * LOG2_E

        @pl.loop(0, HEADS // 4)
        def _(group):
            for i in range(4):
                cols = head_columns(4 * group + i)
                q, k, v = qkv[3 * r, :, cols], qkv[3 * r + 1, :, cols], qkv[3 * r + 2, :, cols]
                s = dot_t(q, k)
                top = jnp.max(s, 1, keepdims=True)
                e = jnp.exp2((s - top) * factor)
                total = jnp.sum(e, 1, keepdims=True)
                lse[r, group, :, i:i + 1] = top * factor + jnp.log2(total)
                factors[mixed + r, :, cols] = (dot(e.astype(BF16), v) * (1.0 / total)).astype(BF16)

        bo_, s2, o2 = vector(4), vector(2), vector(3)
        for part in halves:
            value = xr[r, part, :].astype(F32) + dot(factors[mixed + r, part, :], vo[...]) + bo_
            resid[r, part, :] = value
            hat, _ = norm_parts(value)
            factors[h2 + r, part, :] = (hat * s2 + o2).astype(BF16)
        bu = vector(5)
        for part in halves:
            u = dot(factors[h2 + r, part, :], vu[...]) + bu
            t = jnp.tanh(GELU_A * (u + GELU_B * u * u * u))
            factors[act + r, part, :] = (0.5 * u * (1.0 + t)).astype(BF16)
            back[gp + r, part, :] = (
                0.5 * (1.0 + t) + 0.5 * u * (1.0 - t * t) * (GELU_A * (1.0 + 3.0 * GELU_B * u * u))
            ).astype(BF16)
        bd = vector(6)
        keep = jnp.minimum(crops[place(r, z)], 1).astype(F32)
        for part in halves:
            value = resid[r, part, :] + dot(factors[act + r, part, :], vd[...]) + bd
            bo[r, part, :] = (value * keep).astype(BF16)
        bo_piece(r, 0).start()

    def add_sum(index, value):
        sums[0, index:index + 1, :] = sums[0, index:index + 1, :] + value

    def backward_mlp(r):
        held = crops[place(r, z)]
        share = jnp.full((1, width), jnp.minimum(held, 1).astype(F32)) / jnp.full((1, width), jnp.maximum(held, 1).astype(F32))
        for k in range(lanes):
            arrive(cot_piece, r, k)
            part = pl.ds(k * chunk, chunk)
            g = (cr[r, part, :].astype(F32) * share).astype(BF16)
            back[gl + r, part, :] = g
            add_sum(0, column_sum(g.astype(F32)))
            issue_next(cot_piece, r, k)

        @pl.when(r == last)
        def _():
            for s in range(1, rounds):
                issue(bo_piece, s)

        for part in halves:
            g = (dot_t(back[gl + r, part, :], vd[...]) * back[gp + r, part, :].astype(F32)).astype(BF16)
            back[gp + r, part, :] = g
            add_sum(1, column_sum(g.astype(F32)))
        s2 = vector(2)
        for part in halves:
            gh = dot_t(back[gp + r, part, :], vu[...])
            hat, inverse = norm_parts(resid[r, part, :])
            add_sum(2, column_sum(gh * hat))
            add_sum(3, column_sum(gh))
            value = cr[r, part, :].astype(F32) * share + norm_back(gh * s2, hat, inverse)
            resid[r, part, :] = value
            g = value.astype(BF16)
            back[ga + r, part, :] = g
            add_sum(4, column_sum(g.astype(F32)))
        for part in halves:
            gm[0, part, :] = dot_t(back[ga + r, part, :], vo[...]).astype(BF16)

    def backward_attention(r):
        factor = size ** -0.5

        for h in range(HEADS):
            if h % 4 == 0:
                lse_rows = lse[r, h // 4].T
            cols = slice(h * size, (h + 1) * size)
            q, k, v, m = qkv[3 * r, :, cols], qkv[3 * r + 1, :, cols], qkv[3 * r + 2, :, cols], gm[0, :, cols]
            p = jnp.exp2(dot_t(k, q) * (factor * LOG2_E) - lse_rows[h % 4:h % 4 + 1, :])
            dp = dot_t(v, m)
            ds = (p * (dp - jnp.sum(p * dp, 0, keepdims=True))).astype(BF16)
            qkv[3 * r + 2, :, cols] = dot(p.astype(BF16), m).astype(BF16)
            qkv[3 * r + 1, :, cols] = (dot(ds, q) * factor).astype(BF16)
            qkv[3 * r, :, cols] = (dot(k.T, ds) * factor).T.astype(BF16)

    def backward_input(r):
        s1 = vector(0)
        for part in halves:
            gh = dot_t(qkv[3 * r, part, :], vq[:, :width])
            gh = gh + dot_t(qkv[3 * r + 1, part, :], vq[:, width:2 * width])
            gh = gh + dot_t(qkv[3 * r + 2, part, :], vq[:, 2 * width:])
            hat, inverse = norm_parts(xr[r, part, :].astype(F32))
            add_sum(5, column_sum(gh * hat))
            add_sum(6, column_sum(gh))
            xr[r, part, :] = (resid[r, part, :] + norm_back(gh * s1, hat, inverse)).astype(BF16)

    totals = (summed, factors)
    count = len(steps_left)
    unit = width >> count
    per_half = width // 2 // unit
    sides = (slice(0, width // 2), slice(width // 2, width))

    def spots(steps):
        terms = []
        for i, (axis, bit) in enumerate(steps):
            mine = (img // bit) % 2 if axis == "img" else (z // bit) % 2
            scale = 1 if axis == "row" else (width // unit) // images
            weight = 1 if i == 0 else unit << (count - 1 - i)
            terms.append((bit * scale, (mine * weight, (1 - mine) * weight)))
        found = []
        for block in range(width // unit):
            picked = [pair[(block // divisor) % 2] for divisor, pair in terms]
            found.append((picked[0], pl.multiple_of(sum(picked[2:], picked[1]), unit)))
        return found

    def place_products(total_pages, rounds_of, left, right):
        places_of = [spots(steps_left), spots(steps_right)]
        first_round = rounds_of[0]

        @pl.loop(0, 3)
        def _(c):
            for side, offset in ((0, 0), (1, width // 2)):
                for first_column in range(offset, offset + width // 2, 256):
                    cols = slice(first_column, first_column + 256)
                    total = dot_tt(left(c, first_round), right(c, first_round, cols))
                    for r in rounds_of[1:]:
                        total = total + dot_tt(left(c, r), right(c, r, cols))
                    for block, (goes, first) in enumerate(places_of[side]):
                        rows_of = (c + 3 * goes, pl.ds(first, unit), cols)
                        part = total[block * unit:(block + 1) * unit]
                        if len(rounds_of) == 1:
                            part = part + jnp.where(first_round > 0, total_pages[rows_of].astype(F32), 0.0)
                        total_pages[rows_of] = part.astype(BF16)

    def send(group, step, side):
        steps = (steps_left, steps_right)[side]
        if step == 0:
            source, target = totals[group].at[pl.ds(3, 3)], got_first
        else:
            length = rows >> step
            source = totals[group].at[pl.ds(0, 3), pl.ds(length, length), sides[side]]
            target = got_next.at[:, pl.ds(rows - 2 * length, length), sides[side]]
        return pltpu.make_async_remote_copy(
            src_ref=source, dst_ref=target, send_sem=red_out.at[group, step, side], recv_sem=red_in.at[group, step, side],
            device_id=device(*steps[step]), device_id_type=MESH)

    def begin(group, step, side):
        if group:
            pl.semaphore_wait(credit.at[step, side], 1)
        send(group, step, side).start()

    def reduce_step(group, step):
        length = rows >> step
        middle = length // 2
        for side in (0, 1):
            cols = sides[side]
            if step or side == 0:
                send(group, step, side).wait_recv()

            def added(c, first, extent):
                if step == 0:
                    got = got_first[c, pl.ds(first, extent), cols]
                else:
                    got = got_next[c, pl.ds(rows - 2 * length + first, extent), cols]
                return totals[group][c, pl.ds(first, extent), cols].astype(F32) + got.astype(F32)

            if step == count - 1:
                for c in range(3):
                    first_column = (3 * group + c) * width
                    products_out[:, first_column + cols.start:first_column + cols.stop] = added(c, 0, length)
            else:
                def keep_part(first):
                    @pl.loop(0, 3)
                    def _(c):
                        totals[group][c, pl.ds(first, middle), cols] = added(c, first, middle).astype(BF16)

                keep_part(middle)
                begin(group, step + 1, side)
                keep_part(0)
            if group == 0 and (step or side):
                steps = (steps_left, steps_right)[side]
                pl.semaphore_signal(
                    credit.at[step, side if step else 0], inc=1, device_id=device(*steps[step]), device_id_type=MESH)

    for load in loads:
        load.wait()
    loop_rounds(forward)

    def mlp_products(r):
        place_products(
            summed, [r], lambda c, s: factors[rounds * c + s], lambda c, s, cols: back[rounds * c + s, :, cols])

    @loop_rounds
    def _(r):
        backward_mlp(r)

        @pl.when(r == last)
        def _():
            mlp_products(r)
            begin(0, 0, 0)

        backward_attention(r)

        @pl.when(r == last)
        def _():
            for s in range(last):
                issue(lg_piece, s)
            reduce_step(0, 0)
            place_products(
                factors, range(rounds), lambda c, s: h1[s], lambda c, s, cols: qkv[3 * s + c, :, cols])
            begin(1, 0, 0)

        backward_input(r)
        lg_piece(r, 0).start()

        @pl.when(r < last)
        def _():
            mlp_products(r)


    gates = {count - 3: [2], count - 2: [3], count - 1: [1]} if in_lanes and lanes == 4 else {0: range(1, lanes)}

    def results_out(step):
        for k in gates.get(step, ()):
            lg_piece(last, k).start()

    sum_moves = [
        pltpu.make_async_remote_copy(
            src_ref=sums.at[i], dst_ref=sums_got.at[i], send_sem=sum_out.at[i], recv_sem=sum_in.at[i],
            device_id=device(axis, bit), device_id_type=MESH)
        for i, (axis, bit) in enumerate(steps_left)
    ]
    sum_moves[0].start()
    results_out(0)
    for step in range(1, count + 1):
        if step < count:
            reduce_step(0, step)
        if step == count - 3:
            results_out(step)
        reduce_step(1, step - 1)
        if step > count - 3:
            results_out(step)
        sum_moves[step - 1].wait()
        sums[step] = sums[step - 1] + sums_got[step - 1]
        if step < count:
            sum_moves[step].start()
    sums_out[...] = sums[count]

    for group in (0, 1):
        send(group, 0, 0).wait_send()
        for step in range(1, count):
            for side in (0, 1):
                send(group, step, side).wait_send()
    for r in range(rounds):
        for k in range(1, lanes):
            lat_piece(r, k).wait_send()
            cot_piece(r, k).wait_send()
        for piece in (bo_piece, lg_piece):
            for k in range(lanes):
                piece(r, k).wait()


def local(
    latents, cotangent, slot_crops, ln1_scale, ln1_offset, qkv_weight, out_weight, out_bias,
    ln2_scale, ln2_offset, up_weight, up_bias, down_weight, down_bias,
):
    slots, chunk, width = latents.shape
    images, lanes = lax.axis_size("img"), lax.axis_size("row")
    rounds = slots // lanes
    rows = chunk * lanes
    devices = images * lanes
    image_bits = bits_of(images)
    left = [("img", image_bits[0])] + [("img", b) for b in image_bits[1:]]
    right = [("img", image_bits[0])] + [("img", b) for b in reversed(image_bits[1:])]
    whole_sum = width // devices >= 16
    if whole_sum:
        lane_steps = [("row", b) for b in bits_of(lanes)]
        left, right = left + lane_steps, right + lane_steps
    count = len(left)
    unit = width >> count
    sds = jax.ShapeDtypeStruct
    page = lambda n, kind=BF16: pltpu.VMEM((n, rows, width), kind)
    dma = lambda *shape: pltpu.SemaphoreType.DMA(shape)
    macs = rounds * (rows * width * width * 18 + rows * rows * width * 7)
    results, products, totals = pl.pallas_call(
        functools.partial(block_kernel, images, lanes, slots, left, right, whole_sum),
        out_shape=[sds((2 * slots, chunk, width), BF16), sds((unit, 6 * width), F32), sds((8, width), F32)],
        in_specs=[SM] + [VM] * 7 + [ANY] * 6,
        out_specs=[ANY] + [VM] * 2,
        scratch_shapes=[
            pltpu.VMEM((width, 3 * width), BF16), pltpu.VMEM((width, width), BF16), pltpu.VMEM((width, width), BF16),
            pltpu.VMEM((width, width), BF16),
            page(rounds), page(rounds), page(rounds), page(3 * rounds), page(rounds, F32), page(6), page(max(6, 3 * rounds)),
            page(3 * rounds), page(1), page(rounds),
            pltpu.VMEM((rounds, HEADS // 4, rows, 128), F32),
            pltpu.VMEM((count + 1, 8, width), F32), pltpu.VMEM((count, 8, width), F32),
            page(3), page(3),
            dma(4), dma(4, rounds),
            dma(rounds, lanes), dma(rounds, lanes), dma(rounds, lanes), dma(rounds, lanes),
            dma(rounds, lanes), dma(rounds, lanes), dma(rounds, lanes), dma(rounds, lanes),
            dma(2, count, 2), dma(2, count, 2), pltpu.SemaphoreType.REGULAR((count, 2)), dma(count), dma(count),
        ],
        compiler_params=pltpu.CompilerParams(collective_id=0, has_side_effects=True, vmem_limit_bytes=VMEM_LIMIT),
        cost_estimate=pl.CostEstimate(flops=2 * macs, bytes_accessed=32 << 20, transcendentals=0),
        name="latent_block",
    )(slot_crops, ln1_scale, ln1_offset, ln2_scale, ln2_offset, out_bias, up_bias, down_bias, latents, cotangent, qkv_weight, out_weight, up_weight, down_weight)
    if not whole_sum:
        products = lax.psum_scatter(products, "row", scatter_dimension=0, tiled=True)
        totals = lax.psum(totals, "row")
    down_grad, up_grad, out_grad, qkv_grad = jnp.split(products, (width, 2 * width, 3 * width), 1)
    block_out, latents_grad = results[:slots], results[slots:]
    me = lax.axis_index("img") * lanes + lax.axis_index("row")
    part = width // devices
    mine = lax.dynamic_slice(totals, (0, me * part), (8, part))
    return (
        block_out, latents_grad, mine[5], mine[6], qkv_grad, out_grad, mine[4], mine[2], mine[3], up_grad, mine[1], down_grad,
        mine[0],
    )


def solution(mesh):
    whole, both = P(), P(("img", "row"))
    rows, wide = P("img", "row", None), P(("img", "row"), None)
    in_specs = (rows, rows, P("img")) + (whole,) * 11
    out_specs = (rows, rows, both, both, wide, wide, both, both, both, wide, both, wide, both)
    return jax.shard_map(local, mesh=mesh, in_specs=in_specs, out_specs=out_specs, check_vma=False)
```

```python
import functools
import jax
import jax.numpy as jnp
from jax import lax
from jax.experimental import pallas as pl
from jax.experimental.pallas import tpu as pltpu
from jax.sharding import PartitionSpec as P

HEADS = 8
EPSILON = 1e-05
F32 = jnp.float32
BF16 = jnp.bfloat16
MESH = pl.DeviceIdType.MESH
ANY = pl.BlockSpec(memory_space=pl.ANY)
VM = pl.BlockSpec(memory_space=pltpu.VMEM)
SM = pl.BlockSpec(memory_space=pltpu.SMEM)
GELU_A = 0.7978845608028654
GELU_B = 0.044715
LOG2_E = 1.4426950408889634
EARLY = {1: (3, 2), 3: (1,)}
VMEM_LIMIT = 64 * 1024 * 1024 - 64 * 1024


def dot(a, b):
    return jnp.dot(a, b, preferred_element_type=F32)


def dot_t(a, b):
    return lax.dot_general(a, b, (((1,), (1,)), ((), ())), preferred_element_type=F32)


def dot_tt(a, b):
    return lax.dot_general(a, b, (((0,), (0,)), ((), ())), preferred_element_type=F32)


def norm_parts(values):
    mean = jnp.mean(values, -1, keepdims=True)
    centred = values - mean
    inverse = lax.rsqrt(jnp.mean(centred * centred, -1, keepdims=True) + EPSILON)
    return centred * inverse, inverse


def norm_back(scaled, hat, inverse):
    return inverse * (scaled - jnp.mean(scaled, -1, keepdims=True) - hat * jnp.mean(scaled * hat, -1, keepdims=True))


def column_sum(values):
    return jnp.sum(values, 0, keepdims=True)


def bits_of(extent):
    return [1 << i for i in range(extent.bit_length() - 1)]


def flipped(index, bit):
    return index + bit - 2 * bit * ((index // bit) % 2)


def block_kernel(images, lanes, places, steps_left, steps_right, in_lanes, *refs):
    crops, vectors, (lat, cot), refs = refs[0], refs[1:8], refs[8:10], refs[10:]
    mats, refs = refs[:4], refs[4:]
    (results, products_out, sums_out), refs = refs[:3], refs[3:]
    (vq, vo, vu, vd, xr, cr, h1, qkv, resid, summed, factors, back, gm, bo, lse, sums, sums_got, got_first, got_next), refs = refs[:19], refs[19:]
    (mat_sem, own_sem, lat_out, lat_in, cot_out, cot_in, bo_out, bo_in, lg_out, lg_in,
     red_out, red_in, credit, sum_out, sum_in) = refs
    rounds, rows, width = h1.shape
    chunk = rows // lanes
    size = width // HEADS
    img, z = lax.axis_index("img"), lax.axis_index("row")
    act, h2, mixed = (rounds * i for i in range(3))
    gl, gp, ga = (rounds * i for i in range(3))
    last = rounds - 1

    def device(axis, bit):
        return (flipped(img, bit), z) if axis == "img" else (img, flipped(z, bit))

    def lane(k):
        other = z
        for bit in bits_of(lanes):
            if k & bit:
                other = flipped(other, bit)
        return other

    def place(r, other):
        return r * lanes + other

    def loop_rounds(body):
        pl.loop(0, rounds)(body)

    partners = {(axis, bit) for axis, bit in steps_left} | {("row", bit) for bit in bits_of(lanes)}
    friends = [device(axis, bit) for axis, bit in sorted(partners)]
    friends += [(img, lane(k)) for k in range(1, lanes) if k & (k - 1)]
    barrier = pltpu.get_barrier_semaphore()
    for friend in friends:
        pl.semaphore_signal(barrier, inc=1, device_id=friend, device_id_type=MESH)
    loads = [pltpu.make_async_copy(a, b, mat_sem.at[i]) for i, (a, b) in enumerate(zip(mats, (vq, vo, vu, vd)))]

    def piece_in(source, target, sent, got, own, r, k):
        if k == 0:
            return pltpu.make_async_copy(source.at[place(r, z)], target.at[r, pl.ds(0, chunk)], own_sem.at[own, r])
        return pltpu.make_async_remote_copy(
            src_ref=source.at[place(r, lane(k))], dst_ref=target.at[r, pl.ds(k * chunk, chunk)],
            send_sem=sent.at[r, k], recv_sem=got.at[r, k], device_id=(img, lane(k)), device_id_type=MESH)

    def piece_out(source, first, sent, got, own, r, k):
        target = results.at[first + place(r, z)]
        if k == 0:
            return pltpu.make_async_copy(source.at[r, pl.ds(0, chunk)], target, own_sem.at[own, r])
        return pltpu.make_async_remote_copy(
            src_ref=source.at[r, pl.ds(k * chunk, chunk)], dst_ref=target,
            send_sem=sent.at[r, k], recv_sem=got.at[r, k], device_id=(img, lane(k)), device_id_type=MESH)

    lat_piece = functools.partial(piece_in, lat, xr, lat_out, lat_in, 0)
    cot_piece = functools.partial(piece_in, cot, cr, cot_out, cot_in, 1)
    bo_piece = functools.partial(piece_out, bo, 0, bo_out, bo_in, 2)
    lg_piece = functools.partial(piece_out, xr, places, lg_out, lg_in, 3)

    def arrive(piece, r, k):
        move = piece(r, k)
        move.wait() if k == 0 else move.wait_recv()

    for load in loads:
        load.start()
    for piece in (lat_piece, cot_piece):
        for r in range(rounds):
            piece(r, 0).start()
    sums[...] = jnp.zeros_like(sums)
    pl.semaphore_wait(barrier, len(friends))

    def issue(piece, r):
        for k in range(lanes - 1, 0, -1):
            piece(r, k).start()

    issue(lat_piece, 0)

    def issue_next(piece, r, k):
        for kk in EARLY.get(k, ()):
            @pl.when(r < last)
            def _():
                piece(r + 1, kk).start()

            @pl.when(r == last)
            def _():
                if piece is lat_piece:
                    cot_piece(0, kk).start()
                else:
                    bo_piece(0, kk).start()

    half = rows // 2
    halves = [pl.ds(i * half, half) for i in range(2)]
    vector = lambda i: vectors[i][...].astype(F32).reshape(1, width)

    def head_columns(h):
        return pl.ds(pl.multiple_of(h * size, size), size)

    def forward(r):
        s1, o1 = vector(0), vector(1)
        for k in range(lanes):
            arrive(lat_piece, r, k)
            part = pl.ds(k * chunk, chunk)
            hat, _ = norm_parts(xr[r, part, :].astype(F32))
            h1[r, part, :] = (hat * s1 + o1).astype(BF16)
            issue_next(lat_piece, r, k)

        for n in range(3):
            qkv[3 * r + n] = dot(h1[r], vq[:, n * width:(n + 1) * width]).astype(BF16)
        factor = size ** -0.5 * LOG2_E

        @pl.loop(0, HEADS // 4)
        def _(group):
            for i in range(4):
                cols = head_columns(4 * group + i)
                q, k, v = qkv[3 * r, :, cols], qkv[3 * r + 1, :, cols], qkv[3 * r + 2, :, cols]
                s = dot_t(q, k)
                top = jnp.max(s, 1, keepdims=True)
                e = jnp.exp2((s - top) * factor)
                total = jnp.sum(e, 1, keepdims=True)
                lse[r, group, :, i:i + 1] = top * factor + jnp.log2(total)
                factors[mixed + r, :, cols] = (dot(e.astype(BF16), v) * (1.0 / total)).astype(BF16)

        bo_, s2, o2 = vector(4), vector(2), vector(3)
        for part in halves:
            value = xr[r, part, :].astype(F32) + dot(factors[mixed + r, part, :], vo[...]) + bo_
            resid[r, part, :] = value
            hat, _ = norm_parts(value)
            factors[h2 + r, part, :] = (hat * s2 + o2).astype(BF16)
        bu = vector(5)
        for part in halves:
            u = dot(factors[h2 + r, part, :], vu[...]) + bu
            t = jnp.tanh(GELU_A * (u + GELU_B * u * u * u))
            factors[act + r, part, :] = (0.5 * u * (1.0 + t)).astype(BF16)
            back[gp + r, part, :] = (
                0.5 * (1.0 + t) + 0.5 * u * (1.0 - t * t) * (GELU_A * (1.0 + 3.0 * GELU_B * u * u))
            ).astype(BF16)
        bd = vector(6)
        keep = jnp.minimum(crops[place(r, z)], 1).astype(F32)
        for part in halves:
            value = resid[r, part, :] + dot(factors[act + r, part, :], vd[...]) + bd
            bo[r, part, :] = (value * keep).astype(BF16)
        bo_piece(r, 0).start()

    def add_sum(index, value):
        sums[0, index:index + 1, :] = sums[0, index:index + 1, :] + value

    def backward_mlp(r):
        held = crops[place(r, z)]
        share = jnp.full((1, width), jnp.minimum(held, 1).astype(F32)) / jnp.full((1, width), jnp.maximum(held, 1).astype(F32))
        for k in range(lanes):
            arrive(cot_piece, r, k)
            part = pl.ds(k * chunk, chunk)
            g = (cr[r, part, :].astype(F32) * share).astype(BF16)
            back[gl + r, part, :] = g
            add_sum(0, column_sum(g.astype(F32)))
            issue_next(cot_piece, r, k)

        @pl.when(r == last)
        def _():
            for s in range(1, rounds):
                issue(bo_piece, s)

        for part in halves:
            g = (dot_t(back[gl + r, part, :], vd[...]) * back[gp + r, part, :].astype(F32)).astype(BF16)
            back[gp + r, part, :] = g
            add_sum(1, column_sum(g.astype(F32)))
        s2 = vector(2)
        for part in halves:
            gh = dot_t(back[gp + r, part, :], vu[...])
            hat, inverse = norm_parts(resid[r, part, :])
            add_sum(2, column_sum(gh * hat))
            add_sum(3, column_sum(gh))
            value = cr[r, part, :].astype(F32) * share + norm_back(gh * s2, hat, inverse)
            resid[r, part, :] = value
            g = value.astype(BF16)
            back[ga + r, part, :] = g
            add_sum(4, column_sum(g.astype(F32)))
        for part in halves:
            gm[0, part, :] = dot_t(back[ga + r, part, :], vo[...]).astype(BF16)

    def backward_attention(r):
        factor = size ** -0.5

        for h in range(HEADS):
            if h % 4 == 0:
                lse_rows = lse[r, h // 4].T
            cols = slice(h * size, (h + 1) * size)
            q, k, v, m = qkv[3 * r, :, cols], qkv[3 * r + 1, :, cols], qkv[3 * r + 2, :, cols], gm[0, :, cols]
            p = jnp.exp2(dot_t(k, q) * (factor * LOG2_E) - lse_rows[h % 4:h % 4 + 1, :])
            dp = dot_t(v, m)
            ds = (p * (dp - jnp.sum(p * dp, 0, keepdims=True))).astype(BF16)
            qkv[3 * r + 2, :, cols] = dot(p.astype(BF16), m).astype(BF16)
            qkv[3 * r + 1, :, cols] = (dot(ds, q) * factor).astype(BF16)
            qkv[3 * r, :, cols] = (dot(k.T, ds) * factor).T.astype(BF16)

    def backward_input(r):
        s1 = vector(0)
        for part in halves:
            gh = dot_t(qkv[3 * r, part, :], vq[:, :width])
            gh = gh + dot_t(qkv[3 * r + 1, part, :], vq[:, width:2 * width])
            gh = gh + dot_t(qkv[3 * r + 2, part, :], vq[:, 2 * width:])
            hat, inverse = norm_parts(xr[r, part, :].astype(F32))
            add_sum(5, column_sum(gh * hat))
            add_sum(6, column_sum(gh))
            xr[r, part, :] = (resid[r, part, :] + norm_back(gh * s1, hat, inverse)).astype(BF16)

    totals = (summed, factors)
    count = len(steps_left)
    unit = width >> count
    per_half = width // 2 // unit
    sides = (slice(0, width // 2), slice(width // 2, width))

    def spots(steps):
        terms = []
        for i, (axis, bit) in enumerate(steps):
            mine = (img // bit) % 2 if axis == "img" else (z // bit) % 2
            scale = 1 if axis == "row" else (width // unit) // images
            weight = 1 if i == 0 else unit << (count - 1 - i)
            terms.append((bit * scale, (mine * weight, (1 - mine) * weight)))
        found = []
        for block in range(width // unit):
            picked = [pair[(block // divisor) % 2] for divisor, pair in terms]
            found.append((picked[0], pl.multiple_of(sum(picked[2:], picked[1]), unit)))
        return found

    def place_products(total_pages, rounds_of, left, right):
        places_of = [spots(steps_left), spots(steps_right)]
        first_round = rounds_of[0]

        @pl.loop(0, 3)
        def _(c):
            for side, offset in ((0, 0), (1, width // 2)):
                for first_column in range(offset, offset + width // 2, 256):
                    cols = slice(first_column, first_column + 256)
                    total = dot_tt(left(c, first_round), right(c, first_round, cols))
                    for r in rounds_of[1:]:
                        total = total + dot_tt(left(c, r), right(c, r, cols))
                    for block, (goes, first) in enumerate(places_of[side]):
                        rows_of = (c + 3 * goes, pl.ds(first, unit), cols)
                        part = total[block * unit:(block + 1) * unit]
                        if len(rounds_of) == 1:
                            part = part + jnp.where(first_round > 0, total_pages[rows_of].astype(F32), 0.0)
                        total_pages[rows_of] = part.astype(BF16)

    def send(group, step, side):
        steps = (steps_left, steps_right)[side]
        if step == 0:
            source, target = totals[group].at[pl.ds(3, 3)], got_first
        else:
            length = rows >> step
            source = totals[group].at[pl.ds(0, 3), pl.ds(length, length), sides[side]]
            target = got_next.at[:, pl.ds(rows - 2 * length, length), sides[side]]
        return pltpu.make_async_remote_copy(
            src_ref=source, dst_ref=target, send_sem=red_out.at[group, step, side], recv_sem=red_in.at[group, step, side],
            device_id=device(*steps[step]), device_id_type=MESH)

    def begin(group, step, side):
        if group:
            pl.semaphore_wait(credit.at[step, side], 1)
        send(group, step, side).start()

    def reduce_step(group, step):
        length = rows >> step
        middle = length // 2
        for side in (0, 1):
            cols = sides[side]
            if step or side == 0:
                send(group, step, side).wait_recv()

            def added(c, first, extent):
                if step == 0:
                    got = got_first[c, pl.ds(first, extent), cols]
                else:
                    got = got_next[c, pl.ds(rows - 2 * length + first, extent), cols]
                return totals[group][c, pl.ds(first, extent), cols].astype(F32) + got.astype(F32)

            if step == count - 1:
                for c in range(3):
                    first_column = (3 * group + c) * width
                    products_out[:, first_column + cols.start:first_column + cols.stop] = added(c, 0, length)
            else:
                def keep_part(first):
                    @pl.loop(0, 3)
                    def _(c):
                        totals[group][c, pl.ds(first, middle), cols] = added(c, first, middle).astype(BF16)

                keep_part(middle)
                begin(group, step + 1, side)
                keep_part(0)
            if group == 0 and (step or side):
                steps = (steps_left, steps_right)[side]
                pl.semaphore_signal(
                    credit.at[step, side if step else 0], inc=1, device_id=device(*steps[step]), device_id_type=MESH)

    for load in loads:
        load.wait()
    loop_rounds(forward)

    def mlp_products(r):
        place_products(
            summed, [r], lambda c, s: factors[rounds * c + s], lambda c, s, cols: back[rounds * c + s, :, cols])

    @loop_rounds
    def _(r):
        backward_mlp(r)

        @pl.when(r == last)
        def _():
            mlp_products(r)
            begin(0, 0, 0)

        backward_attention(r)

        @pl.when(r == last)
        def _():
            for s in range(last):
                issue(lg_piece, s)
            reduce_step(0, 0)
            place_products(
                factors, range(rounds), lambda c, s: h1[s], lambda c, s, cols: qkv[3 * s + c, :, cols])
            begin(1, 0, 0)

        backward_input(r)
        lg_piece(r, 0).start()

        @pl.when(r < last)
        def _():
            mlp_products(r)


    gates = {count - 3: [2], count - 2: [3], count - 1: [1]} if in_lanes and lanes == 4 else {0: range(1, lanes)}

    def results_out(step):
        for k in gates.get(step, ()):
            lg_piece(last, k).start()

    sum_moves = [
        pltpu.make_async_remote_copy(
            src_ref=sums.at[i], dst_ref=sums_got.at[i], send_sem=sum_out.at[i], recv_sem=sum_in.at[i],
            device_id=device(axis, bit), device_id_type=MESH)
        for i, (axis, bit) in enumerate(steps_left)
    ]
    sum_moves[0].start()
    results_out(0)
    for step in range(1, count + 1):
        if step < count:
            reduce_step(0, step)
        if step == count - 3:
            results_out(step)
        reduce_step(1, step - 1)
        if step > count - 3:
            results_out(step)
        sum_moves[step - 1].wait()
        sums[step] = sums[step - 1] + sums_got[step - 1]
        if step < count:
            sum_moves[step].start()
    sums_out[...] = sums[count]

    for group in (0, 1):
        send(group, 0, 0).wait_send()
        for step in range(1, count):
            for side in (0, 1):
                send(group, step, side).wait_send()
    for r in range(rounds):
        for k in range(1, lanes):
            lat_piece(r, k).wait_send()
            cot_piece(r, k).wait_send()
        for piece in (bo_piece, lg_piece):
            for k in range(lanes):
                piece(r, k).wait()


def finish_kernel(part, lanes, first, second, products, sums, block_out, latents_grad, down, up, out, qkv, mine):
    block_out[...] = first[...]
    latents_grad[...] = second[...]

    @pl.when(pl.program_id(0) == 0)
    def _():
        width = down.shape[1]
        for i, target in enumerate((down, up, out)):
            target[...] = products[:, i * width:(i + 1) * width]
        qkv[...] = products[:, 3 * width:]
        start = (lax.axis_index("img") * lanes + lax.axis_index("row")) * part
        mine[...] = pltpu.roll(sums[...], (width - start) % width, 1)[:, :128]


def local(
    latents, cotangent, slot_crops, ln1_scale, ln1_offset, qkv_weight, out_weight, out_bias,
    ln2_scale, ln2_offset, up_weight, up_bias, down_weight, down_bias,
):
    slots, chunk, width = latents.shape
    images, lanes = lax.axis_size("img"), lax.axis_size("row")
    rounds = slots // lanes
    rows = chunk * lanes
    devices = images * lanes
    image_bits = bits_of(images)
    left = [("img", image_bits[0])] + [("img", b) for b in image_bits[1:]]
    right = [("img", image_bits[0])] + [("img", b) for b in reversed(image_bits[1:])]
    whole_sum = width // devices >= 16
    if whole_sum:
        lane_steps = [("row", b) for b in bits_of(lanes)]
        left, right = left + lane_steps, right + lane_steps
    count = len(left)
    unit = width >> count
    sds = jax.ShapeDtypeStruct
    page = lambda n, kind=BF16: pltpu.VMEM((n, rows, width), kind)
    dma = lambda *shape: pltpu.SemaphoreType.DMA(shape)
    macs = rounds * (rows * width * width * 18 + rows * rows * width * 7)
    results, products, totals = pl.pallas_call(
        functools.partial(block_kernel, images, lanes, slots, left, right, whole_sum),
        out_shape=[sds((2 * slots, chunk, width), BF16), sds((unit, 6 * width), F32), sds((8, width), F32)],
        in_specs=[SM] + [VM] * 7 + [ANY] * 6,
        out_specs=[ANY] + [VM] * 2,
        scratch_shapes=[
            pltpu.VMEM((width, 3 * width), BF16), pltpu.VMEM((width, width), BF16), pltpu.VMEM((width, width), BF16),
            pltpu.VMEM((width, width), BF16),
            page(rounds), page(rounds), page(rounds), page(3 * rounds), page(rounds, F32), page(6), page(max(6, 3 * rounds)),
            page(3 * rounds), page(1), page(rounds),
            pltpu.VMEM((rounds, HEADS // 4, rows, 128), F32),
            pltpu.VMEM((count + 1, 8, width), F32), pltpu.VMEM((count, 8, width), F32),
            page(3), page(3),
            dma(4), dma(4, rounds),
            dma(rounds, lanes), dma(rounds, lanes), dma(rounds, lanes), dma(rounds, lanes),
            dma(rounds, lanes), dma(rounds, lanes), dma(rounds, lanes), dma(rounds, lanes),
            dma(2, count, 2), dma(2, count, 2), pltpu.SemaphoreType.REGULAR((count, 2)), dma(count), dma(count),
        ],
        compiler_params=pltpu.CompilerParams(collective_id=0, has_side_effects=True, vmem_limit_bytes=VMEM_LIMIT),
        cost_estimate=pl.CostEstimate(flops=2 * macs, bytes_accessed=32 << 20, transcendentals=0),
        name="latent_block",
    )(slot_crops, ln1_scale, ln1_offset, ln2_scale, ln2_offset, out_bias, up_bias, down_bias, latents, cotangent, qkv_weight, out_weight, up_weight, down_weight)
    if not whole_sum:
        products = lax.psum_scatter(products, "row", scatter_dimension=0, tiled=True)
        totals = lax.psum(totals, "row")
    part = width // devices
    steps = 2 if slots % 2 == 0 else 1
    whole = lambda *shape: pl.BlockSpec(shape, lambda i: (0,) * len(shape))
    some = lambda first: pl.BlockSpec((slots // steps, chunk, width), lambda i: (first + i, 0, 0))
    share_rows = products.shape[0]
    block_out, latents_grad, down_grad, up_grad, out_grad, qkv_grad, mine = pl.pallas_call(
        functools.partial(finish_kernel, part, lanes),
        grid=(steps,),
        out_shape=[sds(latents.shape, BF16)] * 2 + [sds((share_rows, width), F32)] * 3
        + [sds((share_rows, 3 * width), F32), sds((8, 128), F32)],
        in_specs=[some(0), some(steps), whole(share_rows, 6 * width), whole(8, width)],
        out_specs=[some(0), some(0)] + [whole(share_rows, width)] * 3 + [whole(share_rows, 3 * width), whole(8, 128)],
        name="results_apart",
    )(results, results, products, totals)
    mine = mine[:, :part]
    return (
        block_out, latents_grad, mine[5], mine[6], qkv_grad, out_grad, mine[4], mine[2], mine[3], up_grad, mine[1], down_grad,
        mine[0],
    )


def solution(mesh):
    whole, both = P(), P(("img", "row"))
    rows, wide = P("img", "row", None), P(("img", "row"), None)
    in_specs = (rows, rows, P("img")) + (whole,) * 11
    out_specs = (rows, rows, both, both, wide, wide, both, both, both, wide, both, wide, both)
    return jax.shard_map(local, mesh=mesh, in_specs=in_specs, out_specs=out_specs, check_vma=False)
```

```python
import functools
import jax
import jax.numpy as jnp
from jax import lax
from jax.experimental import pallas as pl
from jax.experimental.pallas import tpu as pltpu
from jax.sharding import PartitionSpec as P

HEADS = 8
EPSILON = 1e-05
F32 = jnp.float32
BF16 = jnp.bfloat16
MESH = pl.DeviceIdType.MESH
ANY = pl.BlockSpec(memory_space=pl.ANY)
VM = pl.BlockSpec(memory_space=pltpu.VMEM)
SM = pl.BlockSpec(memory_space=pltpu.SMEM)
GELU_A = 0.7978845608028654
GELU_B = 0.044715
LOG2_E = 1.4426950408889634
EARLY = {1: (3, 2), 3: (1,)}
VMEM_LIMIT = 64 * 1024 * 1024 - 64 * 1024


def dot(a, b):
    return jnp.dot(a, b, preferred_element_type=F32)


def dot_t(a, b):
    return lax.dot_general(a, b, (((1,), (1,)), ((), ())), preferred_element_type=F32)


def dot_tt(a, b):
    return lax.dot_general(a, b, (((0,), (0,)), ((), ())), preferred_element_type=F32)


def norm_parts(values):
    mean = jnp.mean(values, -1, keepdims=True)
    centred = values - mean
    inverse = lax.rsqrt(jnp.mean(centred * centred, -1, keepdims=True) + EPSILON)
    return centred * inverse, inverse


def norm_back(scaled, hat, inverse):
    return inverse * (scaled - jnp.mean(scaled, -1, keepdims=True) - hat * jnp.mean(scaled * hat, -1, keepdims=True))


def column_sum(values):
    return jnp.sum(values, 0, keepdims=True)


def bits_of(extent):
    return [1 << i for i in range(extent.bit_length() - 1)]


def flipped(index, bit):
    return index + bit - 2 * bit * ((index // bit) % 2)


def block_kernel(images, lanes, places, steps_left, steps_right, in_lanes, *refs):
    crops, vectors, (lat, cot), refs = refs[0], refs[1:8], refs[8:10], refs[10:]
    mats, refs = refs[:4], refs[4:]
    (results, products_out, sums_out), refs = refs[:3], refs[3:]
    (vq, vo, vu, vd, xr, cr, h1, qkv, resid, summed, factors, back, gm, bo, lse, sums, sums_got, got_first, got_next), refs = refs[:19], refs[19:]
    (mat_sem, own_sem, lat_out, lat_in, cot_out, cot_in, bo_out, bo_in, lg_out, lg_in,
     red_out, red_in, credit, sum_out, sum_in) = refs
    rounds, rows, width = h1.shape
    chunk = rows // lanes
    size = width // HEADS
    img, z = lax.axis_index("img"), lax.axis_index("row")
    act, h2, mixed = (rounds * i for i in range(3))
    gl, gp, ga = (rounds * i for i in range(3))
    last = rounds - 1

    def device(axis, bit):
        return (flipped(img, bit), z) if axis == "img" else (img, flipped(z, bit))

    def lane(k):
        other = z
        for bit in bits_of(lanes):
            if k & bit:
                other = flipped(other, bit)
        return other

    def place(r, other):
        return r * lanes + other

    def loop_rounds(body):
        pl.loop(0, rounds)(body)

    partners = {(axis, bit) for axis, bit in steps_left} | {("row", bit) for bit in bits_of(lanes)}
    friends = [device(axis, bit) for axis, bit in sorted(partners)]
    friends += [(img, lane(k)) for k in range(1, lanes) if k & (k - 1)]
    barrier = pltpu.get_barrier_semaphore()
    for friend in friends:
        pl.semaphore_signal(barrier, inc=1, device_id=friend, device_id_type=MESH)
    loads = [pltpu.make_async_copy(a, b, mat_sem.at[i]) for i, (a, b) in enumerate(zip(mats, (vq, vo, vu, vd)))]

    def piece_in(source, target, sent, got, own, r, k):
        if k == 0:
            return pltpu.make_async_copy(source.at[place(r, z)], target.at[r, pl.ds(0, chunk)], own_sem.at[own, r])
        return pltpu.make_async_remote_copy(
            src_ref=source.at[place(r, lane(k))], dst_ref=target.at[r, pl.ds(k * chunk, chunk)],
            send_sem=sent.at[r, k], recv_sem=got.at[r, k], device_id=(img, lane(k)), device_id_type=MESH)

    def piece_out(source, first, sent, got, own, r, k):
        target = results.at[first + place(r, z)]
        if k == 0:
            return pltpu.make_async_copy(source.at[r, pl.ds(0, chunk)], target, own_sem.at[own, r])
        return pltpu.make_async_remote_copy(
            src_ref=source.at[r, pl.ds(k * chunk, chunk)], dst_ref=target,
            send_sem=sent.at[r, k], recv_sem=got.at[r, k], device_id=(img, lane(k)), device_id_type=MESH)

    lat_piece = functools.partial(piece_in, lat, xr, lat_out, lat_in, 0)
    cot_piece = functools.partial(piece_in, cot, cr, cot_out, cot_in, 1)
    bo_piece = functools.partial(piece_out, bo, 0, bo_out, bo_in, 2)
    lg_piece = functools.partial(piece_out, xr, places, lg_out, lg_in, 3)

    def arrive(piece, r, k):
        move = piece(r, k)
        move.wait() if k == 0 else move.wait_recv()

    for load in loads:
        load.start()
    for piece in (lat_piece, cot_piece):
        for r in range(rounds):
            piece(r, 0).start()
    sums[...] = jnp.zeros_like(sums)
    pl.semaphore_wait(barrier, len(friends))

    def issue(piece, r):
        for k in range(lanes - 1, 0, -1):
            piece(r, k).start()

    issue(lat_piece, 0)

    def issue_next(piece, r, k):
        for kk in EARLY.get(k, ()):
            @pl.when(r < last)
            def _():
                piece(r + 1, kk).start()

            @pl.when(r == last)
            def _():
                if piece is lat_piece:
                    cot_piece(0, kk).start()
                else:
                    bo_piece(0, kk).start()

    half = rows // 2
    halves = [pl.ds(i * half, half) for i in range(2)]
    vector = lambda i: vectors[i][...].astype(F32).reshape(1, width)

    def head_columns(h):
        return pl.ds(pl.multiple_of(h * size, size), size)

    def forward(r):
        s1, o1 = vector(0), vector(1)
        for k in range(lanes):
            arrive(lat_piece, r, k)
            part = pl.ds(k * chunk, chunk)
            hat, _ = norm_parts(xr[r, part, :].astype(F32))
            h1[r, part, :] = (hat * s1 + o1).astype(BF16)
            issue_next(lat_piece, r, k)

        for n in range(3):
            qkv[3 * r + n] = dot(h1[r], vq[:, n * width:(n + 1) * width]).astype(BF16)
        factor = size ** -0.5 * LOG2_E

        @pl.loop(0, HEADS // 4)
        def _(group):
            for i in range(4):
                cols = head_columns(4 * group + i)
                q, k, v = qkv[3 * r, :, cols], qkv[3 * r + 1, :, cols], qkv[3 * r + 2, :, cols]
                s = dot_t(q, k)
                top = jnp.max(s, 1, keepdims=True)
                e = jnp.exp2((s - top) * factor)
                total = jnp.sum(e, 1, keepdims=True)
                lse[r, group, :, i:i + 1] = top * factor + jnp.log2(total)
                factors[mixed + r, :, cols] = (dot(e.astype(BF16), v) * (1.0 / total)).astype(BF16)

        bo_, s2, o2 = vector(4), vector(2), vector(3)
        for part in halves:
            value = xr[r, part, :].astype(F32) + dot(factors[mixed + r, part, :], vo[...]) + bo_
            resid[r, part, :] = value
            hat, _ = norm_parts(value)
            factors[h2 + r, part, :] = (hat * s2 + o2).astype(BF16)
        bu = vector(5)
        for part in halves:
            u = dot(factors[h2 + r, part, :], vu[...]) + bu
            t = jnp.tanh(GELU_A * (u + GELU_B * u * u * u))
            factors[act + r, part, :] = (0.5 * u * (1.0 + t)).astype(BF16)
            back[gp + r, part, :] = (
                0.5 * (1.0 + t) + 0.5 * u * (1.0 - t * t) * (GELU_A * (1.0 + 3.0 * GELU_B * u * u))
            ).astype(BF16)
        bd = vector(6)
        keep = jnp.minimum(crops[place(r, z)], 1).astype(F32)
        for part in halves:
            value = resid[r, part, :] + dot(factors[act + r, part, :], vd[...]) + bd
            bo[r, part, :] = (value * keep).astype(BF16)
        bo_piece(r, 0).start()

    def add_sum(index, value):
        sums[0, index:index + 1, :] = sums[0, index:index + 1, :] + value

    def backward_mlp(r):
        held = crops[place(r, z)]
        share = jnp.full((1, width), jnp.minimum(held, 1).astype(F32)) / jnp.full((1, width), jnp.maximum(held, 1).astype(F32))
        for k in range(lanes):
            arrive(cot_piece, r, k)
            part = pl.ds(k * chunk, chunk)
            g = (cr[r, part, :].astype(F32) * share).astype(BF16)
            back[gl + r, part, :] = g
            add_sum(0, column_sum(g.astype(F32)))
            issue_next(cot_piece, r, k)

        @pl.when(r == last)
        def _():
            for s in range(1, rounds):
                issue(bo_piece, s)

        for part in halves:
            g = (dot_t(back[gl + r, part, :], vd[...]) * back[gp + r, part, :].astype(F32)).astype(BF16)
            back[gp + r, part, :] = g
            add_sum(1, column_sum(g.astype(F32)))
        s2 = vector(2)
        for part in halves:
            gh = dot_t(back[gp + r, part, :], vu[...])
            hat, inverse = norm_parts(resid[r, part, :])
            add_sum(2, column_sum(gh * hat))
            add_sum(3, column_sum(gh))
            value = cr[r, part, :].astype(F32) * share + norm_back(gh * s2, hat, inverse)
            resid[r, part, :] = value
            g = value.astype(BF16)
            back[ga + r, part, :] = g
            add_sum(4, column_sum(g.astype(F32)))
        for part in halves:
            gm[0, part, :] = dot_t(back[ga + r, part, :], vo[...]).astype(BF16)

    def backward_attention(r):
        factor = size ** -0.5

        for h in range(HEADS):
            if h % 4 == 0:
                lse_rows = lse[r, h // 4].T
            cols = slice(h * size, (h + 1) * size)
            q, k, v, m = qkv[3 * r, :, cols], qkv[3 * r + 1, :, cols], qkv[3 * r + 2, :, cols], gm[0, :, cols]
            p = jnp.exp2(dot_t(k, q) * (factor * LOG2_E) - lse_rows[h % 4:h % 4 + 1, :])
            dp = dot_t(v, m)
            ds = (p * (dp - jnp.sum(p * dp, 0, keepdims=True))).astype(BF16)
            qkv[3 * r + 2, :, cols] = dot(p.astype(BF16), m).astype(BF16)
            qkv[3 * r + 1, :, cols] = (dot(ds, q) * factor).astype(BF16)
            qkv[3 * r, :, cols] = (dot(k.T, ds) * factor).T.astype(BF16)

    def backward_input(r):
        s1 = vector(0)
        for part in halves:
            gh = dot_t(qkv[3 * r, part, :], vq[:, :width])
            gh = gh + dot_t(qkv[3 * r + 1, part, :], vq[:, width:2 * width])
            gh = gh + dot_t(qkv[3 * r + 2, part, :], vq[:, 2 * width:])
            hat, inverse = norm_parts(xr[r, part, :].astype(F32))
            add_sum(5, column_sum(gh * hat))
            add_sum(6, column_sum(gh))
            xr[r, part, :] = (resid[r, part, :] + norm_back(gh * s1, hat, inverse)).astype(BF16)

    totals = (summed, factors)
    count = len(steps_left)
    unit = width >> count
    per_half = width // 2 // unit
    sides = (slice(0, width // 2), slice(width // 2, width))

    def spots(steps):
        terms = []
        for i, (axis, bit) in enumerate(steps):
            mine = (img // bit) % 2 if axis == "img" else (z // bit) % 2
            scale = 1 if axis == "row" else (width // unit) // images
            weight = 1 if i == 0 else unit << (count - 1 - i)
            terms.append((bit * scale, (mine * weight, (1 - mine) * weight)))
        found = []
        for block in range(width // unit):
            picked = [pair[(block // divisor) % 2] for divisor, pair in terms]
            found.append((picked[0], pl.multiple_of(sum(picked[2:], picked[1]), unit)))
        return found

    def place_products(total_pages, rounds_of, left, right):
        places_of = [spots(steps_left), spots(steps_right)]
        first_round = rounds_of[0]

        @pl.loop(0, 3)
        def _(c):
            for side, offset in ((0, 0), (1, width // 2)):
                for first_column in range(offset, offset + width // 2, 256):
                    cols = slice(first_column, first_column + 256)
                    total = dot_tt(left(c, first_round), right(c, first_round, cols))
                    for r in rounds_of[1:]:
                        total = total + dot_tt(left(c, r), right(c, r, cols))
                    for block, (goes, first) in enumerate(places_of[side]):
                        rows_of = (c + 3 * goes, pl.ds(first, unit), cols)
                        part = total[block * unit:(block + 1) * unit]
                        if len(rounds_of) == 1:
                            part = part + jnp.where(first_round > 0, total_pages[rows_of].astype(F32), 0.0)
                        total_pages[rows_of] = part.astype(BF16)

    def send(group, step, side):
        steps = (steps_left, steps_right)[side]
        if step == 0:
            source, target = totals[group].at[pl.ds(3, 3)], got_first
        else:
            length = rows >> step
            source = totals[group].at[pl.ds(0, 3), pl.ds(length, length), sides[side]]
            target = got_next.at[:, pl.ds(rows - 2 * length, length), sides[side]]
        return pltpu.make_async_remote_copy(
            src_ref=source, dst_ref=target, send_sem=red_out.at[group, step, side], recv_sem=red_in.at[group, step, side],
            device_id=device(*steps[step]), device_id_type=MESH)

    def begin(group, step, side):
        if group:
            pl.semaphore_wait(credit.at[step, side], 1)
        send(group, step, side).start()

    def reduce_step(group, step):
        length = rows >> step
        middle = length // 2
        for side in (0, 1):
            cols = sides[side]
            if step or side == 0:
                send(group, step, side).wait_recv()

            def added(c, first, extent):
                if step == 0:
                    got = got_first[c, pl.ds(first, extent), cols]
                else:
                    got = got_next[c, pl.ds(rows - 2 * length + first, extent), cols]
                return totals[group][c, pl.ds(first, extent), cols].astype(F32) + got.astype(F32)

            if step == count - 1:
                for c in range(3):
                    first_column = (3 * group + c) * width
                    products_out[:, first_column + cols.start:first_column + cols.stop] = added(c, 0, length)
            else:
                def keep_part(first):
                    @pl.loop(0, 3)
                    def _(c):
                        totals[group][c, pl.ds(first, middle), cols] = added(c, first, middle).astype(BF16)

                keep_part(middle)
                begin(group, step + 1, side)
                keep_part(0)
            if group == 0 and (step or side):
                steps = (steps_left, steps_right)[side]
                pl.semaphore_signal(
                    credit.at[step, side if step else 0], inc=1, device_id=device(*steps[step]), device_id_type=MESH)

    for load in loads:
        load.wait()
    loop_rounds(forward)

    def mlp_products(r):
        place_products(
            summed, [r], lambda c, s: factors[rounds * c + s], lambda c, s, cols: back[rounds * c + s, :, cols])

    @loop_rounds
    def _(r):
        backward_mlp(r)

        @pl.when(r == last)
        def _():
            mlp_products(r)
            begin(0, 0, 0)

        backward_attention(r)

        @pl.when(r == last)
        def _():
            for s in range(last):
                issue(lg_piece, s)
            reduce_step(0, 0)
            place_products(
                factors, range(rounds), lambda c, s: h1[s], lambda c, s, cols: qkv[3 * s + c, :, cols])
            begin(1, 0, 0)

        backward_input(r)
        lg_piece(r, 0).start()

        @pl.when(r < last)
        def _():
            mlp_products(r)


    gates = {count - 3: [2, 1], count - 2: [3]} if in_lanes and lanes == 4 else {0: range(1, lanes)}

    def results_out(step):
        for k in gates.get(step, ()):
            lg_piece(last, k).start()

    sum_moves = [
        pltpu.make_async_remote_copy(
            src_ref=sums.at[i], dst_ref=sums_got.at[i], send_sem=sum_out.at[i], recv_sem=sum_in.at[i],
            device_id=device(axis, bit), device_id_type=MESH)
        for i, (axis, bit) in enumerate(steps_left)
    ]
    sum_moves[0].start()
    results_out(0)
    for step in range(1, count + 1):
        if step < count:
            reduce_step(0, step)
        if step == count - 3:
            results_out(step)
        reduce_step(1, step - 1)
        if step > count - 3:
            results_out(step)
        sum_moves[step - 1].wait()
        sums[step] = sums[step - 1] + sums_got[step - 1]
        if step < count:
            sum_moves[step].start()
    sums_out[...] = sums[count]

    for group in (0, 1):
        send(group, 0, 0).wait_send()
        for step in range(1, count):
            for side in (0, 1):
                send(group, step, side).wait_send()
    for r in range(rounds):
        for k in range(1, lanes):
            lat_piece(r, k).wait_send()
            cot_piece(r, k).wait_send()
        for piece in (bo_piece, lg_piece):
            for k in range(lanes):
                piece(r, k).wait()


def finish_kernel(part, lanes, first, second, products, sums, block_out, latents_grad, down, up, out, qkv, mine):
    block_out[...] = first[...]
    latents_grad[...] = second[...]

    @pl.when(pl.program_id(0) == 0)
    def _():
        width = down.shape[1]
        for i, target in enumerate((down, up, out)):
            target[...] = products[:, i * width:(i + 1) * width]
        qkv[...] = products[:, 3 * width:]
        start = (lax.axis_index("img") * lanes + lax.axis_index("row")) * part
        mine[...] = pltpu.roll(sums[...], (width - start) % width, 1)[:, :128]


def local(
    latents, cotangent, slot_crops, ln1_scale, ln1_offset, qkv_weight, out_weight, out_bias,
    ln2_scale, ln2_offset, up_weight, up_bias, down_weight, down_bias,
):
    slots, chunk, width = latents.shape
    images, lanes = lax.axis_size("img"), lax.axis_size("row")
    rounds = slots // lanes
    rows = chunk * lanes
    devices = images * lanes
    image_bits = bits_of(images)
    left = [("img", image_bits[0])] + [("img", b) for b in image_bits[1:]]
    right = [("img", image_bits[0])] + [("img", b) for b in reversed(image_bits[1:])]
    whole_sum = width // devices >= 16
    if whole_sum:
        lane_steps = [("row", b) for b in bits_of(lanes)]
        left, right = left + lane_steps, right + lane_steps
    count = len(left)
    unit = width >> count
    sds = jax.ShapeDtypeStruct
    page = lambda n, kind=BF16: pltpu.VMEM((n, rows, width), kind)
    dma = lambda *shape: pltpu.SemaphoreType.DMA(shape)
    macs = rounds * (rows * width * width * 18 + rows * rows * width * 7)
    results, products, totals = pl.pallas_call(
        functools.partial(block_kernel, images, lanes, slots, left, right, whole_sum),
        out_shape=[sds((2 * slots, chunk, width), BF16), sds((unit, 6 * width), F32), sds((8, width), F32)],
        in_specs=[SM] + [VM] * 7 + [ANY] * 6,
        out_specs=[ANY] + [VM] * 2,
        scratch_shapes=[
            pltpu.VMEM((width, 3 * width), BF16), pltpu.VMEM((width, width), BF16), pltpu.VMEM((width, width), BF16),
            pltpu.VMEM((width, width), BF16),
            page(rounds), page(rounds), page(rounds), page(3 * rounds), page(rounds, F32), page(6), page(max(6, 3 * rounds)),
            page(3 * rounds), page(1), page(rounds),
            pltpu.VMEM((rounds, HEADS // 4, rows, 128), F32),
            pltpu.VMEM((count + 1, 8, width), F32), pltpu.VMEM((count, 8, width), F32),
            page(3), page(3),
            dma(4), dma(4, rounds),
            dma(rounds, lanes), dma(rounds, lanes), dma(rounds, lanes), dma(rounds, lanes),
            dma(rounds, lanes), dma(rounds, lanes), dma(rounds, lanes), dma(rounds, lanes),
            dma(2, count, 2), dma(2, count, 2), pltpu.SemaphoreType.REGULAR((count, 2)), dma(count), dma(count),
        ],
        compiler_params=pltpu.CompilerParams(collective_id=0, has_side_effects=True, vmem_limit_bytes=VMEM_LIMIT),
        cost_estimate=pl.CostEstimate(flops=2 * macs, bytes_accessed=32 << 20, transcendentals=0),
        name="latent_block",
    )(slot_crops, ln1_scale, ln1_offset, ln2_scale, ln2_offset, out_bias, up_bias, down_bias, latents, cotangent, qkv_weight, out_weight, up_weight, down_weight)
    if not whole_sum:
        products = lax.psum_scatter(products, "row", scatter_dimension=0, tiled=True)
        totals = lax.psum(totals, "row")
    part = width // devices
    steps = 2 if slots % 2 == 0 else 1
    whole = lambda *shape: pl.BlockSpec(shape, lambda i: (0,) * len(shape))
    some = lambda first: pl.BlockSpec((slots // steps, chunk, width), lambda i: (first + i, 0, 0))
    share_rows = products.shape[0]
    block_out, latents_grad, down_grad, up_grad, out_grad, qkv_grad, mine = pl.pallas_call(
        functools.partial(finish_kernel, part, lanes),
        grid=(steps,),
        out_shape=[sds(latents.shape, BF16)] * 2 + [sds((share_rows, width), F32)] * 3
        + [sds((share_rows, 3 * width), F32), sds((8, 128), F32)],
        in_specs=[some(0), some(steps), whole(share_rows, 6 * width), whole(8, width)],
        out_specs=[some(0), some(0)] + [whole(share_rows, width)] * 3 + [whole(share_rows, 3 * width), whole(8, 128)],
        name="results_apart",
    )(results, results, products, totals)
    mine = mine[:, :part]
    return (
        block_out, latents_grad, mine[5], mine[6], qkv_grad, out_grad, mine[4], mine[2], mine[3], up_grad, mine[1], down_grad,
        mine[0],
    )


def solution(mesh):
    whole, both = P(), P(("img", "row"))
    rows, wide = P("img", "row", None), P(("img", "row"), None)
    in_specs = (rows, rows, P("img")) + (whole,) * 11
    out_specs = (rows, rows, both, both, wide, wide, both, both, both, wide, both, wide, both)
    return jax.shard_map(local, mesh=mesh, in_specs=in_specs, out_specs=out_specs, check_vma=False)
```
